1024 devices in a mesh: dp: 64 (over z, core), expert: 16 (over y, x).
Axes of the slice: x: 4, y: 4, z: 32, core: 2. Of those that a mesh axis runs over, the one named last changes fastest.
Arguments:
- tokens: bfloat16 [131072, 1024], P(('dp', 'expert')), may hold values from -24 to 24
- gate_weight: bfloat16 [16, 1024, 768], P('expert'), may hold values from -0.1875 to 0.1875
- up_weight: bfloat16 [16, 1024, 768], P('expert'), may hold values from -0.1875 to 0.1875
- hidden_grad: bfloat16 [64, 16, 256, 768], P('dp', 'expert'), may hold values from -6 to 6
- chosen: int32 [64, 16, 256], P('dp', 'expert'), may hold values from 0 to 2047, as said below
- routes: int32 [131072, 4], P(('dp', 'expert')), may hold values from 0 to 4095, as said below
- route_count: int32 [131072], P(('dp', 'expert')), may hold values from 0 to 4, as said below
Outputs:
- token_grad: bfloat16 [131072, 1024], P(('dp', 'expert'))
- grad_gate: float32 [16, 1024, 768], P('expert', 'dp')
- grad_up: float32 [16, 1024, 768], P('expert', 'dp')
The draws below stay inside these ranges and needn't reach their ends.
Inputs may be any that keep to these rules, and one draw needn't show every extreme that they name: Each row chosen[g, e] lists 256 different tokens of the group in increasing order; at most 32 of them lie among the 128 tokens of one device, and in every group one device's tokens give exactly 32 to every expert. `routes`: the first route_count[t] entries of token t are the codes e * 256 + k with chosen[g, e, k] = t, in increasing order, each slot once; the other entries are 0. `route_count`: among the tokens of one device the counts differ by at most one; some token has 4.
All inputs are finite; a program needn't handle non-finite values.
Results may differ from the reference program's by a relative error of at most 0.01.
Values may be sent and summed in bfloat16 or wider, within the bound.
No kernel may reach another device: no remote copies, remote signals or barrier semaphores. Data moves between devices by JAX's collectives and lax.ppermute only.
A program may use at most 32 MiB of HBM per device.

```python
from functools import partial
import jax
import jax.numpy as jnp
from jax import lax

D = 1024
FF = 768
TOK_DEV = 128
EXPERTS = 16
GROUPS = 64
SLOTS = 256
PEER_CAP = 32
RMAX = 4
TOKENS = 131072


def group_layout(group_key):
    hot_key, order_key, shift_key, token_key = jax.random.split(group_key, 4)
    sources = EXPERTS
    hot_source = jax.random.randint(hot_key, (), 0, sources)
    remaining = SLOTS - PEER_CAP
    others = sources - 1
    base_count = remaining // others
    leftover = remaining - base_count * others
    ordered = base_count + (jnp.arange(others) < leftover).astype(jnp.int32)
    ordered = jnp.broadcast_to(ordered, (EXPERTS, others)).astype(jnp.int32)
    pair_count = others // 2
    first_half = ordered[:, 0:2 * pair_count:2]
    second_half = ordered[:, 1:2 * pair_count:2]
    limit = jnp.minimum(jnp.minimum(first_half, second_half), PEER_CAP - jnp.maximum(first_half, second_half))
    moved = jax.random.randint(shift_key, (EXPERTS, pair_count), -limit, limit + 1).astype(jnp.int32)
    ordered = ordered.at[:, 0:2 * pair_count:2].add(moved)
    ordered = ordered.at[:, 1:2 * pair_count:2].add(-moved)
    shuffles = jax.vmap(partial(jax.random.permutation, x=others))(jax.random.split(order_key, EXPERTS))
    shuffled = jnp.take_along_axis(ordered, shuffles.astype(jnp.int32), axis=1)
    other_sources = ((hot_source + 1 + jnp.arange(others)) % sources).astype(jnp.int32)
    counts = jnp.zeros((EXPERTS, sources), jnp.int32).at[:, other_sources].set(shuffled)
    counts = counts.at[:, hot_source].set(PEER_CAP)
    before_expert = jnp.cumsum(counts, axis=0) - counts
    ends = jnp.cumsum(counts, axis=1)
    starts = ends - counts
    slot_index = jnp.arange(SLOTS, dtype=jnp.int32)
    source_of = jnp.sum((ends[:, None, :] <= slot_index[None, :, None]).astype(jnp.int32), axis=2)
    start_of = jnp.take_along_axis(starts, source_of, axis=1)
    offset_of = jnp.take_along_axis(before_expert, source_of, axis=1)
    position = (offset_of + slot_index[None, :] - start_of) % TOK_DEV
    token_perms = jax.vmap(partial(jax.random.permutation, x=TOK_DEV))(jax.random.split(token_key, sources)).astype(jnp.int32)
    local_token = token_perms[source_of, position]
    chosen = jnp.sort(source_of * TOK_DEV + local_token, axis=1).astype(jnp.int32)
    group_tokens = EXPERTS * TOK_DEV
    flat_tokens = chosen.reshape(-1)
    route_codes = jnp.arange(EXPERTS * SLOTS, dtype=jnp.int32)
    sort_order = jnp.argsort(flat_tokens, stable=True)
    sorted_tokens = flat_tokens[sort_order]
    sorted_codes = route_codes[sort_order]
    first_index = jnp.searchsorted(sorted_tokens, sorted_tokens, side='left').astype(jnp.int32)
    route_rank = jnp.arange(EXPERTS * SLOTS, dtype=jnp.int32) - first_index
    routes = jnp.zeros((group_tokens, RMAX), jnp.int32).at[sorted_tokens, route_rank].set(sorted_codes)
    token_tally = jnp.zeros((group_tokens,), jnp.int32).at[flat_tokens].add(1)
    return (chosen, routes, token_tally)


def full_layout(key):
    group_keys = jax.random.split(key, GROUPS)
    chosen, routes, token_tally = jax.vmap(group_layout)(group_keys)
    return (chosen, routes.reshape(TOKENS, RMAX), token_tally.reshape(TOKENS))


def draw_chosen(key, part):
    return full_layout(key)[0]


def draw_routes(key, part):
    return full_layout(key)[1]


def draw_route_count(key, part):
    return full_layout(key)[2]


def spiked(entries, key, source, target, shards_of, factor):
    def block_of(axis_at):
        return (jnp.arange(entries.shape[axis_at]) // (entries.shape[axis_at] // shards_of)).reshape((-1,) + (1,) * (entries.ndim - 1 - axis_at))

    near = jax.random.permutation(key, shards_of)[block_of(target)]
    far = (block_of(target) + shards_of // 2) % shards_of
    return jnp.where((block_of(source) == near) | (block_of(source) == far), factor * entries, entries)


def levels(stream_key, shape, cuts, low, largest):
    gain = 1.0
    for axis_at, parts in cuts:
        heights = jax.random.uniform(jax.random.fold_in(jax.random.fold_in(stream_key, 6), axis_at), (parts,), jnp.float32, low / len(cuts), largest / len(cuts))
        gain = gain * jnp.repeat(jnp.exp(heights), shape[axis_at] // parts).reshape((-1,) + (1,) * (len(shape) - 1 - axis_at))
    return gain


def normal_values(own_key, extent, spread, most, shards=(), kind=jnp.bfloat16):
    values = spread * jax.random.normal(own_key, extent, jnp.float32)
    if shards:
        values = values * levels(own_key, extent, shards, -0.22, 0.18)
    return jnp.clip(values, -most, most).astype(kind)


def heavy_noise(own_key, shape, scale, reach, shards, heavy, kind=jnp.bfloat16):
    array = scale * jax.random.normal(own_key, shape, jnp.float32)
    if shards:
        array = array * levels(own_key, shape, shards, -0.22, 0.18)
    return jnp.clip(spiked(array, jax.random.fold_in(own_key, 3), *heavy), -reach, reach).astype(kind)


def setup_inputs(seed: int = 0) -> dict:
    streams_of = jax.random.split(jax.random.key(seed), 8)
    tokens = heavy_noise(streams_of[0], (TOKENS, D), 1.0, 24.0, ((0, 1024),), (0, 1, 1024, 6.0))
    gate_weight = normal_values(streams_of[1], (EXPERTS, D, FF), D ** -0.5, 0.1875, ((0, 16),))
    up_weight = normal_values(streams_of[2], (EXPERTS, D, FF), D ** -0.5, 0.1875, ((0, 16),))
    hidden_grad = normal_values(streams_of[3], (GROUPS, EXPERTS, SLOTS, FF), 1.0, 6.0, ((0, 64), (1, 16)))
    chosen = draw_chosen(jax.random.fold_in(streams_of[7], 71), 0)
    routes = draw_routes(jax.random.fold_in(streams_of[7], 71), 0)
    route_count = draw_route_count(jax.random.fold_in(streams_of[7], 71), 0)
    return {"tokens": tokens, "gate_weight": gate_weight, "up_weight": up_weight, "hidden_grad": hidden_grad, "chosen": chosen, "routes": routes, "route_count": route_count}


def silu_parts(pre_gate):
    squash = jax.nn.sigmoid(pre_gate)
    return (pre_gate * squash, squash * (1.0 + pre_gate * (1.0 - squash)))

def expert_backward(inputs):
    picked_rows, gate_matrix, up_matrix, hidden_cot = inputs
    gate_value = jnp.dot(picked_rows, gate_matrix, preferred_element_type=jnp.float32)
    up_value = jnp.dot(picked_rows, up_matrix, preferred_element_type=jnp.float32)
    activated, slope_value = silu_parts(gate_value)
    upstream = hidden_cot.astype(jnp.float32)
    gate_delta = (upstream * up_value * slope_value).astype(jnp.bfloat16)
    up_delta = (upstream * activated).astype(jnp.bfloat16)
    contraction = (((1,), (1,)), ((), ()))
    slot_grad = (lax.dot_general(gate_delta, gate_matrix, contraction, preferred_element_type=jnp.float32) + lax.dot_general(up_delta, up_matrix, contraction, preferred_element_type=jnp.float32)).astype(jnp.bfloat16)
    combined = jnp.concatenate([gate_delta, up_delta], axis=1)
    weight_grad = lax.dot_general(picked_rows, combined, (((0,), (0,)), ((), ())), preferred_element_type=jnp.float32)
    return (slot_grad, weight_grad)

def reference(tokens, gate_weight, up_weight, hidden_grad, chosen, routes, route_count):
    group_tokens = EXPERTS * TOK_DEV

    def one_group(running, bundle):
        shard_tokens, hidden_cot, picked, route_codes, counts = bundle
        gathered_rows = jnp.take(shard_tokens, picked, axis=0)
        slot_grad, weight_grad = lax.map(expert_backward, (gathered_rows, gate_weight, up_weight, hidden_cot))
        flat_grads = slot_grad.reshape(EXPERTS * SLOTS, D).astype(jnp.float32)
        is_live = (jnp.arange(RMAX)[None, :] < counts[:, None]).astype(jnp.float32)
        selected = jnp.take(flat_grads, route_codes, axis=0) * is_live[:, :, None]
        token_grad = lax.optimization_barrier(jnp.sum(selected, axis=1)).astype(jnp.bfloat16)
        return (running + weight_grad, token_grad)
    initial = jnp.zeros((EXPERTS, D, 2 * FF), jnp.float32)
    running, token_grad = lax.scan(one_group, initial, (tokens.reshape(GROUPS, group_tokens, D), hidden_grad, chosen, routes.reshape(GROUPS, group_tokens, RMAX), route_count.reshape(GROUPS, group_tokens)))
    running = running / jnp.sqrt(jnp.float32(GROUPS * SLOTS))
    return (token_grad.reshape(TOKENS, D), running[:, :, :FF], running[:, :, FF:])
```

```python
import functools

import jax
import jax.numpy as jnp
from jax import lax
from jax.experimental import pallas as pl
from jax.experimental.pallas import tpu as pltpu
from jax.sharding import PartitionSpec as P

FAN = 4


def iota(shape, dim):
    return lax.broadcasted_iota(jnp.int32, shape, dim)


def place_rows(member, cap):
    n, m = member.shape
    ones = member.astype(jnp.float32).astype(jnp.bfloat16)
    before = (iota((m, m), 0) < iota((m, m), 1)).astype(jnp.float32).astype(jnp.bfloat16)
    rank = jnp.dot(ones, before, preferred_element_type=jnp.float32)
    rank = jnp.where(member, rank, -1.0).astype(jnp.int32)
    marks = rank[:, None, :] == iota((n, cap, m), 1)
    return marks.astype(jnp.float32).reshape(n * cap, m).astype(jnp.bfloat16)


def token_marks(routes, count, experts, cap, slots):
    depth, tokens = routes.shape
    rows = iota((experts, tokens), 0)
    member = jnp.zeros((experts, tokens), jnp.int32)
    for r in range(depth):
        owner = jnp.where(count > r, lax.div(routes[r : r + 1], jnp.int32(slots)), -1)
        member = member + (owner == rows).astype(jnp.int32)
    return place_rows(member > 0, cap)


def slot_marks(chosen, sources, cap, tokens):
    source = lax.div(chosen, jnp.int32(tokens))
    return place_rows(source == iota((sources, chosen.shape[1]), 0), cap)


def contract(a, b, dims):
    return lax.dot_general(a, b, (dims, ((), ())), preferred_element_type=jnp.float32)


def dispatch_kernel(experts, cap, slots, tokens_ref, routes_ref, count_ref, out_ref):
    marks = token_marks(routes_ref[...], count_ref[...], experts, cap, slots)
    out_ref[...] = jnp.dot(marks, tokens_ref[...], preferred_element_type=jnp.float32).astype(jnp.bfloat16)


def combine_kernel(experts, cap, slots, back_ref, routes_ref, count_ref, out_ref):
    marks = token_marks(routes_ref[...], count_ref[...], experts, cap, slots)
    out_ref[...] = contract(marks, back_ref[...], ((0,), (0,))).astype(jnp.bfloat16)


def delta_kernel(sources, cap, tokens, arrived_ref, chosen_ref, order_ref, gate_ref, up_ref, grad_ref, mine_ref, send_ref):
    ff = gate_ref.shape[1]
    width = arrived_ref.shape[1]
    half = width // 2
    marks = slot_marks(chosen_ref[...], sources, cap, tokens)
    rows = contract(marks, arrived_ref[...], ((0,), (0,))).astype(jnp.bfloat16)
    gate = jnp.dot(rows, gate_ref[...], preferred_element_type=jnp.float32)
    up = jnp.dot(rows, up_ref[...], preferred_element_type=jnp.float32)
    squash = jax.nn.sigmoid(gate)
    upstream = grad_ref[...].astype(jnp.float32)
    send_ref[:, half : half + ff] = (upstream * up * (squash * (1.0 + gate * (1.0 - squash)))).astype(jnp.bfloat16)
    send_ref[:, half + ff :] = (upstream * (gate * squash)).astype(jnp.bfloat16)
    pick = (iota((width, width), 0) == order_ref[...]).astype(jnp.float32).astype(jnp.bfloat16)
    ordered = jnp.dot(rows, pick, preferred_element_type=jnp.float32).astype(jnp.bfloat16)
    mine_ref[...] = ordered[:, :half]
    send_ref[:, :half] = ordered[:, half:]


def back_kernel(sources, cap, tokens, half, send_ref, chosen_ref, gate_ref, up_ref, out_ref):
    ff = gate_ref.shape[1]
    grad = contract(send_ref[:, half : half + ff], gate_ref[...], ((1,), (1,)))
    grad = grad + contract(send_ref[:, half + ff :], up_ref[...], ((1,), (1,)))
    marks = slot_marks(chosen_ref[...], sources, cap, tokens)
    out_ref[...] = jnp.dot(marks, grad.astype(jnp.bfloat16), preferred_element_type=jnp.float32).astype(jnp.bfloat16)


def weight_kernel(rows, mine_ref, send_ref, got_ref, keep_ref, next_ref, past_ref, far_ref, near_ref):
    half = mine_ref.shape[1]
    block = half // FAN
    ff = (send_ref.shape[1] - half) // 2

    def part(q):
        cols = slice(q * block, (q + 1) * block)
        own = contract(mine_ref[:, cols], send_ref[:, half:], ((0,), (0,)))
        return own + contract(got_ref[:, cols], got_ref[:, half:], ((0,), (0,)))

    two = part(2).astype(jnp.bfloat16)
    far_ref[...] = two[:, :ff]
    near_ref[:rows] = two[block - rows :, ff:]
    near_ref[rows:] = two[: block - rows, ff:]
    next_ref[...] = part(1).astype(jnp.bfloat16)
    past_ref[...] = part(3).astype(jnp.bfloat16)
    keep_ref[...] = part(0)


def call(kernel, outs, *args):
    shapes = [jax.ShapeDtypeStruct(*o) for o in outs]
    return pl.pallas_call(
        kernel,
        out_shape=shapes if len(shapes) > 1 else shapes[0],
        compiler_params=pltpu.CompilerParams(vmem_limit_bytes=40 * 2**20),
    )(*args)


def on_device(tokens, gate_weight, up_weight, hidden_grad, chosen, routes, route_count):
    tok_dev, width = tokens.shape
    slots, ff = hidden_grad.shape[2:]
    peers = lax.axis_size("expert")
    groups = lax.axis_size("dp")
    cap = min(tok_dev, 2 * slots // peers)
    chips = groups // 2
    rows = width // groups
    half = width // 2
    bf16, f32 = jnp.bfloat16, jnp.float32
    place = lax.axis_index("dp")
    z, core = place // 2, place % 2

    def along(value, hops):
        return lax.ppermute(value, "dp", [(i, (i + 2 * hops) % groups) for i in range(groups)])

    routes_t = routes.T
    count = route_count[None, :]
    picked = chosen[0]
    gate, up = gate_weight[0], up_weight[0]

    outgoing = call(functools.partial(dispatch_kernel, peers, cap, slots), [((peers * cap, width), bf16)], tokens, routes_t, count)
    arrived = lax.all_to_all(
        outgoing.reshape(peers, cap, width), "expert", split_axis=0, concat_axis=0, tiled=True
    ).reshape(peers * cap, width)

    m = jnp.arange(width, dtype=jnp.int32)
    block = half // FAN
    which, q, i = m // half, (m % half) // block, (m % block) // rows
    ahead = FAN * i + jnp.where(q == FAN - 1, -1, q)
    owner = (z + ahead + chips) % chips * 2 + jnp.where(which == 0, core, 1 - core)
    order = (owner * rows + m % rows)[None, :]

    mine, send = call(
        functools.partial(delta_kernel, peers, cap, tok_dev),
        [((slots, half), bf16), ((slots, half + 2 * ff), bf16)],
        arrived, picked, order, gate, up, hidden_grad[0, 0],
    )
    got = lax.ppermute(send, "dp", [(d, d ^ 1) for d in range(groups)])
    back = call(
        functools.partial(back_kernel, peers, cap, tok_dev, half), [((peers * cap, width), bf16)], send, picked, gate, up
    )
    keep, ahead_1, past_1, ahead_2, past_2 = call(
        functools.partial(weight_kernel, rows),
        [((block, 2 * ff), f32), ((block, 2 * ff), bf16), ((block, 2 * ff), bf16), ((block, ff), bf16), ((block, ff), bf16)],
        mine, send, got,
    )
    from_far = along(ahead_2, 2)
    from_near = along(past_2, -2)
    from_1 = along(ahead_1, 1)
    from_past = along(past_1, -1)
    part = keep + from_1.astype(f32) + from_past.astype(f32)
    part = part + jnp.concatenate([from_far, from_near], axis=1).astype(f32)

    returned = lax.all_to_all(
        back.reshape(peers, cap, width), "expert", split_axis=0, concat_axis=0, tiled=True
    ).reshape(peers * cap, width)

    part = part.reshape(chips // FAN, rows, 2 * ff)
    n = chips // FAN
    h = n // 2
    right = part[h].astype(bf16)
    left = part[n - h + 1].astype(bf16)
    for t in range(1, h + 1):
        right = along(right, FAN)
        if t < h:
            right = (right.astype(f32) + part[h - t]).astype(bf16)
            left = along(left, -FAN)
            if t < h - 1:
                left = (left.astype(f32) + part[n - h + 1 + t]).astype(bf16)
    summed = (part[0] + right.astype(f32) + left.astype(f32)) / jnp.sqrt(f32(groups * slots))

    token_grad = call(
        functools.partial(combine_kernel, peers, cap, slots), [((tok_dev, width), bf16)], returned, routes_t, count
    )
    return token_grad, summed[None, :, :ff], summed[None, :, ff:]


def solution(mesh):
    return jax.shard_map(
        on_device,
        mesh=mesh,
        in_specs=(
            P(("dp", "expert"), None),
            P("expert", None, None),
            P("expert", None, None),
            P("dp", "expert", None, None),
            P("dp", "expert", None),
            P(("dp", "expert"), None),
            P(("dp", "expert")),
        ),
        out_specs=(P(("dp", "expert"), None), P("expert", "dp", None), P("expert", "dp", None)),
        check_vma=False,
    )
```

```python
import functools

import jax
import jax.numpy as jnp
from jax import lax
from jax.experimental import pallas as pl
from jax.experimental.pallas import tpu as pltpu
from jax.sharding import PartitionSpec as P

FAN = 4
TIE = 2
BLOCKS = 4


def iota(shape, dim):
    return lax.broadcasted_iota(jnp.int32, shape, dim)


def place_rows(member, cap):
    n, m = member.shape
    ones = member.astype(jnp.float32).astype(jnp.bfloat16)
    before = (iota((m, m), 0) < iota((m, m), 1)).astype(jnp.float32).astype(jnp.bfloat16)
    rank = jnp.dot(ones, before, preferred_element_type=jnp.float32)
    rank = jnp.where(member, rank, -1.0).astype(jnp.int32)
    marks = rank[:, None, :] == iota((n, cap, m), 1)
    return marks.astype(jnp.float32).reshape(n * cap, m).astype(jnp.bfloat16)


def token_marks(routes, count, experts, cap, slots):
    depth, tokens = routes.shape
    rows = iota((experts, tokens), 0)
    member = jnp.zeros((experts, tokens), jnp.int32)
    for r in range(depth):
        owner = jnp.where(count > r, lax.div(routes[r : r + 1], jnp.int32(slots)), -1)
        member = member + (owner == rows).astype(jnp.int32)
    return place_rows(member > 0, cap)


def slot_marks(chosen, sources, cap, tokens):
    source = lax.div(chosen, jnp.int32(tokens))
    return place_rows(source == iota((sources, chosen.shape[1]), 0), cap)


def contract(a, b, dims):
    return lax.dot_general(a, b, (dims, ((), ())), preferred_element_type=jnp.float32)


def fetch(pairs, sems):
    copies = [pltpu.make_async_copy(src, dst, sems.at[i]) for i, (src, dst) in enumerate(pairs)]
    for copy in copies:
        copy.start()
    return copies


def marked_rows(marks, rows, out_ref, stage_ref, sems):
    size = marks.shape[0] // BLOCKS
    copies = []
    for i in range(BLOCKS):
        span = pl.ds(i * size, size)
        block = jnp.dot(marks[i * size : (i + 1) * size], rows, preferred_element_type=jnp.float32)
        stage_ref[span] = block.astype(jnp.bfloat16)
        copies.append(pltpu.make_async_copy(stage_ref.at[span], out_ref.at[span], sems.at[i]))
        copies[-1].start()
    for copy in copies:
        copy.wait()


def dispatch_kernel(experts, cap, slots, tokens_hbm, routes_hbm, count_hbm, out_ref, tokens_ref, routes_ref, count_ref, stage_ref, in_sems, out_sems):
    tokens_in, routes_in, count_in = fetch(
        [(tokens_hbm, tokens_ref), (routes_hbm, routes_ref), (count_hbm, count_ref)], in_sems
    )
    routes_in.wait()
    count_in.wait()
    marks = token_marks(routes_ref[...], count_ref[...], experts, cap, slots)
    tokens_in.wait()
    marked_rows(marks, tokens_ref[...], out_ref, stage_ref, out_sems)


def combine_kernel(experts, cap, slots, back_ref, routes_ref, count_ref, out_ref):
    marks = token_marks(routes_ref[...], count_ref[...], experts, cap, slots)
    out_ref[...] = contract(marks, back_ref[...], ((0,), (0,))).astype(jnp.bfloat16)


def delta_kernel(sources, cap, tokens, arrived_ref, chosen_ref, order_ref, gate_hbm, up_hbm, grad_hbm, mine_ref, send_ref, gate_ref, up_ref, grad_ref, sems):
    ff = gate_ref.shape[1]
    width = arrived_ref.shape[1]
    half = width // 2
    gate_in, up_in, grad_in = fetch([(gate_hbm, gate_ref), (up_hbm, up_ref), (grad_hbm, grad_ref)], sems)
    marks = slot_marks(chosen_ref[...], sources, cap, tokens)
    rows = contract(marks, arrived_ref[...], ((0,), (0,))).astype(jnp.bfloat16)
    pick = (iota((width, width), 0) == order_ref[...]).astype(jnp.float32).astype(jnp.bfloat16)
    gate_in.wait()
    gate = jnp.dot(rows, gate_ref[...], preferred_element_type=jnp.float32)
    up_in.wait()
    up = jnp.dot(rows, up_ref[...], preferred_element_type=jnp.float32)
    squash = jax.nn.sigmoid(gate)
    grad_in.wait()
    upstream = grad_ref[...].astype(jnp.float32)
    send_ref[:, half : half + ff] = (upstream * up * (squash * (1.0 + gate * (1.0 - squash)))).astype(jnp.bfloat16)
    send_ref[:, half + ff :] = (upstream * (gate * squash)).astype(jnp.bfloat16)
    ordered = jnp.dot(rows, pick, preferred_element_type=jnp.float32).astype(jnp.bfloat16)
    mine_ref[...] = ordered[:, :half]
    send_ref[:, :half] = ordered[:, half:]


def back_kernel(sources, cap, tokens, half, send_ref, chosen_ref, gate_ref, up_ref, after_ref, out_ref, stage_ref, sems):
    del after_ref
    ff = gate_ref.shape[1]
    grad = contract(send_ref[:, half : half + ff], gate_ref[...], ((1,), (1,)))
    grad = grad + contract(send_ref[:, half + ff :], up_ref[...], ((1,), (1,)))
    marks = slot_marks(chosen_ref[...], sources, cap, tokens)
    marked_rows(marks, grad.astype(jnp.bfloat16), out_ref, stage_ref, sems)


def weight_kernel(mine_ref, send_ref, got_ref, keep_ref, next_ref, past_ref, far_ref):
    half = mine_ref.shape[1]
    block = half // FAN

    def part(q):
        cols = slice(q * block, (q + 1) * block)
        own = contract(mine_ref[:, cols], send_ref[:, half:], ((0,), (0,)))
        return own + contract(got_ref[:, cols], got_ref[:, half:], ((0,), (0,)))

    far_ref[...] = part(2).astype(jnp.bfloat16)
    next_ref[...] = part(1).astype(jnp.bfloat16)
    past_ref[...] = part(3).astype(jnp.bfloat16)
    keep_ref[...] = part(0)


def call(kernel, outs, *args, ins=None, out_space=None, scratch=(), mib=40):
    shapes = [jax.ShapeDtypeStruct(*o) for o in outs]
    spaces = [s or pltpu.VMEM for s in (ins or [None] * len(args))]
    out_specs = [pl.BlockSpec(memory_space=out_space or pltpu.VMEM) for _ in shapes]
    return pl.pallas_call(
        kernel,
        in_specs=[pl.BlockSpec(memory_space=s) for s in spaces],
        out_specs=out_specs if len(shapes) > 1 else out_specs[0],
        out_shape=shapes if len(shapes) > 1 else shapes[0],
        scratch_shapes=list(scratch),
        compiler_params=pltpu.CompilerParams(vmem_limit_bytes=mib * 2**20),
    )(*args)


def on_device(tokens, gate_weight, up_weight, hidden_grad, chosen, routes, route_count):
    tok_dev, width = tokens.shape
    slots, ff = hidden_grad.shape[2:]
    peers = lax.axis_size("expert")
    groups = lax.axis_size("dp")
    cap = min(tok_dev, 2 * slots // peers)
    chips = groups // 2
    rows = width // groups
    half = width // 2
    bf16, f32 = jnp.bfloat16, jnp.float32
    place = lax.axis_index("dp")
    z, core = place // 2, place % 2

    def along(value, hops):
        pairs = [(d, ((d // 2 + (hops if d % 2 == 0 else -hops)) % chips) * 2 + d % 2) for d in range(groups)]
        return lax.ppermute(value, "dp", pairs)

    routes_t = routes.T
    count = route_count[None, :]
    picked = chosen[0]
    gate, up = gate_weight[0], up_weight[0]
    hbm, vmem, dma = pltpu.HBM, pltpu.VMEM, pltpu.SemaphoreType.DMA
    padded = peers * cap

    outgoing = call(
        functools.partial(dispatch_kernel, peers, cap, slots),
        [((padded, width), bf16)],
        tokens, routes_t, count,
        ins=[hbm] * 3,
        out_space=hbm,
        scratch=[
            vmem(tokens.shape, bf16), vmem(routes_t.shape, jnp.int32), vmem(count.shape, jnp.int32),
            vmem((padded, width), bf16), dma((3,)), dma((BLOCKS,)),
        ],
        mib=61,
    )
    arrived = lax.all_to_all(
        outgoing.reshape(peers, cap, width), "expert", split_axis=0, concat_axis=0, tiled=True
    ).reshape(padded, width)

    m = jnp.arange(width, dtype=jnp.int32)
    block = half // FAN
    which, q, i = m // half, (m % half) // block, (m % block) // rows
    ahead = FAN * i + jnp.where(q == FAN - 1, -1, q)
    to_core = jnp.where(which == 0, core, 1 - core)
    owner = (z + jnp.where(to_core == 0, ahead, -ahead) + 2 * chips) % chips * 2 + to_core
    order = (owner * rows + m % rows)[None, :]

    mine, send = call(
        functools.partial(delta_kernel, peers, cap, tok_dev),
        [((slots, half), bf16), ((slots, half + 2 * ff), bf16)],
        arrived, picked, order, gate, up, hidden_grad[0, 0],
        ins=[None] * 3 + [hbm] * 3,
        scratch=[vmem(gate.shape, bf16), vmem(up.shape, bf16), vmem((slots, ff), bf16), dma((3,))],
        mib=50,
    )
    got = lax.ppermute(send, "dp", [(d, d ^ 1) for d in range(groups)])
    keep, ahead_1, past_1, ahead_2 = call(
        weight_kernel,
        [((block, 2 * ff), f32)] + [((block, 2 * ff), bf16)] * 3,
        mine, send, got,
    )
    back = call(
        functools.partial(back_kernel, peers, cap, tok_dev, half),
        [((padded, width), bf16)],
        send, picked, gate, up, keep,
        ins=[None] * 4 + [pl.ANY],
        out_space=hbm,
        scratch=[vmem((padded, width), bf16), dma((BLOCKS,))],
        mib=40,
    )
    from_2 = along(ahead_2, 2)
    from_1 = along(ahead_1, 1)
    from_past = along(past_1, -1)
    returned = lax.all_to_all(
        back.reshape(peers, cap, width), "expert", split_axis=0, concat_axis=0, tiled=True
    )
    part = keep + from_1.astype(f32) + from_past.astype(f32) + from_2.astype(f32)
    part = part.reshape(chips // FAN, rows, 2 * ff)
    n = chips // FAN
    h = n // 2
    right = part[h].astype(bf16)
    left = part[n - h + 1].astype(bf16)
    for t in range(1, h + 1):
        right = along(right, FAN)
        if t < h:
            left = along(left, -FAN)
            if t == TIE:
                right, left, returned = lax.optimization_barrier((right, left, returned))
            else:
                right, left = lax.optimization_barrier((right, left))
            right = (right.astype(f32) + part[h - t]).astype(bf16)
            if t < h - 1:
                left = (left.astype(f32) + part[n - h + 1 + t]).astype(bf16)
    summed = (part[0] + right.astype(f32) + left.astype(f32)) / jnp.sqrt(f32(groups * slots))

    token_grad = call(
        functools.partial(combine_kernel, peers, cap, slots),
        [((tok_dev, width), bf16)],
        returned.reshape(padded, width), routes_t, count,
    )
    return token_grad, summed[None, :, :ff], summed[None, :, ff:]


def solution(mesh):
    return jax.shard_map(
        on_device,
        mesh=mesh,
        in_specs=(
            P(("dp", "expert"), None),
            P("expert", None, None),
            P("expert", None, None),
            P("dp", "expert", None, None),
            P("dp", "expert", None),
            P(("dp", "expert"), None),
            P(("dp", "expert")),
        ),
        out_specs=(P(("dp", "expert"), None), P("expert", "dp", None), P("expert", "dp", None)),
        check_vma=False,
    )
```

```python
import functools

import jax
import jax.numpy as jnp
from jax import lax
from jax.experimental import pallas as pl
from jax.experimental.pallas import tpu as pltpu
from jax.sharding import PartitionSpec as P

FAN = 4
TIE = 3
BLOCKS = 4


def iota(shape, dim):
    return lax.broadcasted_iota(jnp.int32, shape, dim)


def place_rows(member, cap):
    n, m = member.shape
    ones = member.astype(jnp.float32).astype(jnp.bfloat16)
    before = (iota((m, m), 0) < iota((m, m), 1)).astype(jnp.float32).astype(jnp.bfloat16)
    rank = jnp.dot(ones, before, preferred_element_type=jnp.float32)
    rank = jnp.where(member, rank, -1.0).astype(jnp.int32)
    marks = rank[:, None, :] == iota((n, cap, m), 1)
    return marks.astype(jnp.float32).reshape(n * cap, m).astype(jnp.bfloat16)


def token_marks(routes, count, experts, cap, slots):
    depth, tokens = routes.shape
    rows = iota((experts, tokens), 0)
    member = jnp.zeros((experts, tokens), jnp.int32)
    for r in range(depth):
        owner = jnp.where(count > r, lax.div(routes[r : r + 1], jnp.int32(slots)), -1)
        member = member + (owner == rows).astype(jnp.int32)
    return place_rows(member > 0, cap)


def slot_marks(chosen, sources, cap, tokens):
    source = lax.div(chosen, jnp.int32(tokens))
    return place_rows(source == iota((sources, chosen.shape[1]), 0), cap)


def contract(a, b, dims):
    return lax.dot_general(a, b, (dims, ((), ())), preferred_element_type=jnp.float32)


def fetch(pairs, sems):
    copies = [pltpu.make_async_copy(src, dst, sems.at[i]) for i, (src, dst) in enumerate(pairs)]
    for copy in copies:
        copy.start()
    return copies


def marked_rows(marks, rows, out_ref, stage_ref, sems):
    size = marks.shape[0] // BLOCKS
    copies = []
    for i in range(BLOCKS):
        span = pl.ds(i * size, size)
        block = jnp.dot(marks[i * size : (i + 1) * size], rows, preferred_element_type=jnp.float32)
        stage_ref[span] = block.astype(jnp.bfloat16)
        copies.append(pltpu.make_async_copy(stage_ref.at[span], out_ref.at[span], sems.at[i]))
        copies[-1].start()
    for copy in copies:
        copy.wait()


def dispatch_kernel(experts, cap, slots, tokens_hbm, routes_hbm, count_hbm, out_ref, tokens_ref, routes_ref, count_ref, stage_ref, in_sems, out_sems):
    tokens_in, routes_in, count_in = fetch(
        [(tokens_hbm, tokens_ref), (routes_hbm, routes_ref), (count_hbm, count_ref)], in_sems
    )
    routes_in.wait()
    count_in.wait()
    marks = token_marks(routes_ref[...], count_ref[...], experts, cap, slots)
    tokens_in.wait()
    marked_rows(marks, tokens_ref[...], out_ref, stage_ref, out_sems)


def combine_kernel(experts, cap, slots, back_ref, routes_ref, count_ref, out_ref):
    marks = token_marks(routes_ref[...], count_ref[...], experts, cap, slots)
    out_ref[...] = contract(marks, back_ref[...], ((0,), (0,))).astype(jnp.bfloat16)


def select_kernel(sources, cap, tokens, chosen_ref, order_ref, marks_ref, pick_ref):
    marks_ref[...] = slot_marks(chosen_ref[...], sources, cap, tokens)
    pick_ref[...] = (iota(pick_ref.shape, 0) == order_ref[...]).astype(jnp.float32).astype(jnp.bfloat16)


def delta_kernel(arrived_ref, marks_ref, gate_hbm, up_hbm, grad_hbm, pick_hbm, mine_ref, send_ref, gate_ref, up_ref, grad_ref, pick_ref, sems):
    ff = gate_ref.shape[1]
    half = arrived_ref.shape[1] // 2
    gate_in, up_in, grad_in, pick_in = fetch(
        [(gate_hbm, gate_ref), (up_hbm, up_ref), (grad_hbm, grad_ref), (pick_hbm, pick_ref)], sems
    )
    rows = contract(marks_ref[...], arrived_ref[...], ((0,), (0,))).astype(jnp.bfloat16)
    gate_in.wait()
    gate = jnp.dot(rows, gate_ref[...], preferred_element_type=jnp.float32)
    up_in.wait()
    up = jnp.dot(rows, up_ref[...], preferred_element_type=jnp.float32)
    squash = jax.nn.sigmoid(gate)
    grad_in.wait()
    upstream = grad_ref[...].astype(jnp.float32)
    send_ref[:, half : half + ff] = (upstream * up * (squash * (1.0 + gate * (1.0 - squash)))).astype(jnp.bfloat16)
    send_ref[:, half + ff :] = (upstream * (gate * squash)).astype(jnp.bfloat16)
    pick_in.wait()
    ordered = jnp.dot(rows, pick_ref[...], preferred_element_type=jnp.float32).astype(jnp.bfloat16)
    mine_ref[...] = ordered[:, :half]
    send_ref[:, :half] = ordered[:, half:]


def back_kernel(half, send_ref, marks_ref, gate_hbm, up_hbm, out_ref, gate_ref, up_ref, stage_ref, in_sems, out_sems):
    ff = gate_ref.shape[1]
    gate_in, up_in = fetch([(gate_hbm, gate_ref), (up_hbm, up_ref)], in_sems)
    gate_in.wait()
    grad = contract(send_ref[:, half : half + ff], gate_ref[...], ((1,), (1,)))
    up_in.wait()
    grad = grad + contract(send_ref[:, half + ff :], up_ref[...], ((1,), (1,)))
    marked_rows(marks_ref[...], grad.astype(jnp.bfloat16), out_ref, stage_ref, out_sems)


def weight_kernel(mine_ref, send_ref, got_ref, after_ref, keep_ref, next_ref, past_ref, far_ref):
    del after_ref
    half = mine_ref.shape[1]
    block = half // FAN

    def part(q):
        cols = slice(q * block, (q + 1) * block)
        own = contract(mine_ref[:, cols], send_ref[:, half:], ((0,), (0,)))
        return own + contract(got_ref[:, cols], got_ref[:, half:], ((0,), (0,)))

    far_ref[...] = part(2).astype(jnp.bfloat16)
    next_ref[...] = part(1).astype(jnp.bfloat16)
    past_ref[...] = part(3).astype(jnp.bfloat16)
    keep_ref[...] = part(0)


def call(kernel, outs, *args, ins=None, out_space=None, scratch=(), mib=40):
    shapes = [jax.ShapeDtypeStruct(*o) for o in outs]
    spaces = [s or pltpu.VMEM for s in (ins or [None] * len(args))]
    out_specs = [pl.BlockSpec(memory_space=out_space or pltpu.VMEM) for _ in shapes]
    return pl.pallas_call(
        kernel,
        in_specs=[pl.BlockSpec(memory_space=s) for s in spaces],
        out_specs=out_specs if len(shapes) > 1 else out_specs[0],
        out_shape=shapes if len(shapes) > 1 else shapes[0],
        scratch_shapes=list(scratch),
        compiler_params=pltpu.CompilerParams(vmem_limit_bytes=mib * 2**20),
    )(*args)


def on_device(tokens, gate_weight, up_weight, hidden_grad, chosen, routes, route_count):
    tok_dev, width = tokens.shape
    slots, ff = hidden_grad.shape[2:]
    peers = lax.axis_size("expert")
    groups = lax.axis_size("dp")
    cap = min(tok_dev, 2 * slots // peers)
    chips = groups // 2
    rows = width // groups
    half = width // 2
    bf16, f32 = jnp.bfloat16, jnp.float32
    place = lax.axis_index("dp")
    z, core = place // 2, place % 2

    def along(value, hops):
        pairs = [(d, ((d // 2 + (hops if d % 2 == 0 else -hops)) % chips) * 2 + d % 2) for d in range(groups)]
        return lax.ppermute(value, "dp", pairs)

    def swap(value):
        return lax.ppermute(value, "dp", [(d, d ^ 1) for d in range(groups)])

    n = chips // 2 // FAN
    routes_t = routes.T
    count = route_count[None, :]
    picked = chosen[0]
    gate, up = gate_weight[0], up_weight[0]
    hbm, vmem, dma = pltpu.HBM, pltpu.VMEM, pltpu.SemaphoreType.DMA
    padded = peers * cap

    outgoing = call(
        functools.partial(dispatch_kernel, peers, cap, slots),
        [((padded, width), bf16)],
        tokens, routes_t, count,
        ins=[hbm] * 3,
        out_space=hbm,
        scratch=[
            vmem(tokens.shape, bf16), vmem(routes_t.shape, jnp.int32), vmem(count.shape, jnp.int32),
            vmem((padded, width), bf16), dma((3,)), dma((BLOCKS,)),
        ],
        mib=61,
    )
    arrived = lax.all_to_all(
        outgoing.reshape(peers, cap, width), "expert", split_axis=0, concat_axis=0, tiled=True
    ).reshape(padded, width)

    m = jnp.arange(width, dtype=jnp.int32)
    block = half // FAN
    which, q, i = m // half, (m % half) // block, (m % block) // (2 * rows)
    to_core = jnp.where(which == 0, core, 1 - core)
    last = jnp.where(to_core == 0, chips // 2, 0)
    ahead = jnp.where(q > 0, FAN * i + q, jnp.where(i == n - 1, last, FAN * (i + 1)))
    owner = (z + jnp.where(to_core == 0, ahead, -ahead) + chips) % chips
    order = (owner * 2 * rows + m % (2 * rows))[None, :]
    marks, pick = call(
        functools.partial(select_kernel, peers, cap, tok_dev),
        [((padded, slots), bf16), ((width, width), bf16)],
        picked, order,
        mib=60,
    )

    mine, send = call(
        delta_kernel,
        [((slots, half), bf16), ((slots, half + 2 * ff), bf16)],
        arrived, marks, gate, up, hidden_grad[0, 0], pick,
        ins=[None] * 2 + [hbm] * 4,
        scratch=[vmem(gate.shape, bf16), vmem(up.shape, bf16), vmem((slots, ff), bf16), vmem(pick.shape, bf16), dma((4,))],
        mib=50,
    )
    got = swap(send)
    back = call(
        functools.partial(back_kernel, half),
        [((padded, width), bf16)],
        send, marks, gate, up,
        ins=[None] * 2 + [hbm] * 2,
        out_space=hbm,
        scratch=[vmem(gate.shape, bf16), vmem(up.shape, bf16), vmem((padded, width), bf16), dma((2,)), dma((BLOCKS,))],
        mib=50,
    )
    keep, to_1, to_past, to_2 = call(
        weight_kernel,
        [((block, 2 * ff), f32)] + [((block, 2 * ff), bf16)] * 3,
        mine, send, got, back,
        ins=[None] * 3 + [pl.ANY],
        mib=40,
    )
    from_2, from_1, from_past = [
        v.reshape(n, 2 * rows, 2 * ff).astype(f32) for v in (along(to_2, 2), along(to_1, 1), along(to_past, -1))
    ]
    own = keep.reshape(n, 2 * rows, 2 * ff)
    terms = [from_1[0] + from_2[0] + jnp.where(core == 1, own[n - 1], 0.0)]
    terms += [own[a - 1] + from_1[a] + from_2[a] + from_past[a - 1] for a in range(1, n)]
    total = from_past[n - 1] + jnp.where(core == 0, own[n - 1], 0.0)
    total = total.astype(bf16)
    total, back = lax.optimization_barrier((total, back))
    returned = lax.all_to_all(back.reshape(peers, cap, width), "expert", split_axis=0, concat_axis=0, tiled=True)
    for t in range(1, n + 1):
        total = along(total, FAN)
        if t == TIE:
            total, returned = lax.optimization_barrier((total, returned))
        total = total.astype(f32) + terms[n - t]
        total = total.astype(bf16) if t < n else total
    low, high = total[:rows], total[rows:]
    other = swap(jnp.where(core == 0, high, low).astype(bf16))
    summed = (jnp.where(core == 0, low, high) + other.astype(f32)) / jnp.sqrt(f32(groups * slots))

    token_grad = call(
        functools.partial(combine_kernel, peers, cap, slots),
        [((tok_dev, width), bf16)],
        returned.reshape(padded, width), routes_t, count,
    )
    return token_grad, summed[None, :, :ff], summed[None, :, ff:]


def solution(mesh):
    return jax.shard_map(
        on_device,
        mesh=mesh,
        in_specs=(
            P(("dp", "expert"), None),
            P("expert", None, None),
            P("expert", None, None),
            P("dp", "expert", None, None),
            P("dp", "expert", None),
            P(("dp", "expert"), None),
            P(("dp", "expert")),
        ),
        out_specs=(P(("dp", "expert"), None), P("expert", "dp", None), P("expert", "dp", None)),
        check_vma=False,
    )
```

```python
import functools

import jax
import jax.numpy as jnp
from jax import lax
from jax.experimental import pallas as pl
from jax.experimental.pallas import tpu as pltpu
from jax.sharding import PartitionSpec as P

FAN = 4
TIE = 3
BLOCKS = 4


def iota(shape, dim):
    return lax.broadcasted_iota(jnp.int32, shape, dim)


def place_rows(member, cap):
    n, m = member.shape
    ones = member.astype(jnp.float32).astype(jnp.bfloat16)
    before = (iota((m, m), 0) < iota((m, m), 1)).astype(jnp.float32).astype(jnp.bfloat16)
    rank = jnp.dot(ones, before, preferred_element_type=jnp.float32)
    rank = jnp.where(member, rank, -1.0).astype(jnp.int32)
    marks = rank[:, None, :] == iota((n, cap, m), 1)
    return marks.astype(jnp.float32).reshape(n * cap, m).astype(jnp.bfloat16)


def token_marks(routes, count, experts, cap, slots):
    depth, tokens = routes.shape
    rows = iota((experts, tokens), 0)
    member = jnp.zeros((experts, tokens), jnp.int32)
    for r in range(depth):
        owner = jnp.where(count > r, lax.div(routes[r : r + 1], jnp.int32(slots)), -1)
        member = member + (owner == rows).astype(jnp.int32)
    return place_rows(member > 0, cap)


def slot_marks(chosen, sources, cap, tokens):
    source = lax.div(chosen, jnp.int32(tokens))
    return place_rows(source == iota((sources, chosen.shape[1]), 0), cap)


def contract(a, b, dims):
    return lax.dot_general(a, b, (dims, ((), ())), preferred_element_type=jnp.float32)


def fetch(pairs, sems):
    copies = [pltpu.make_async_copy(src, dst, sems.at[i]) for i, (src, dst) in enumerate(pairs)]
    for copy in copies:
        copy.start()
    return copies


def marked_rows(marks, rows, out_ref, stage_ref, sems):
    size = marks.shape[0] // BLOCKS
    copies = []
    for i in range(BLOCKS):
        span = pl.ds(i * size, size)
        block = jnp.dot(marks[i * size : (i + 1) * size], rows, preferred_element_type=jnp.float32)
        stage_ref[span] = block.astype(jnp.bfloat16)
        copies.append(pltpu.make_async_copy(stage_ref.at[span], out_ref.at[span], sems.at[i]))
        copies[-1].start()
    for copy in copies:
        copy.wait()


def dispatch_kernel(experts, cap, slots, tokens_hbm, routes_hbm, count_hbm, out_ref, tokens_ref, routes_ref, count_ref, stage_ref, in_sems, out_sems):
    tokens_in, routes_in, count_in = fetch(
        [(tokens_hbm, tokens_ref), (routes_hbm, routes_ref), (count_hbm, count_ref)], in_sems
    )
    routes_in.wait()
    count_in.wait()
    marks = token_marks(routes_ref[...], count_ref[...], experts, cap, slots)
    tokens_in.wait()
    marked_rows(marks, tokens_ref[...], out_ref, stage_ref, out_sems)


def combine_kernel(experts, cap, slots, back_ref, routes_ref, count_ref, out_ref):
    marks = token_marks(routes_ref[...], count_ref[...], experts, cap, slots)
    out_ref[...] = contract(marks, back_ref[...], ((0,), (0,))).astype(jnp.bfloat16)


def delta_kernel(sources, cap, tokens, arrived_ref, chosen_ref, order_ref, gate_hbm, up_hbm, grad_hbm, mine_ref, send_ref, gate_ref, up_ref, grad_ref, sems):
    ff = gate_ref.shape[1]
    width = arrived_ref.shape[1]
    half = width // 2
    gate_in, up_in, grad_in = fetch([(gate_hbm, gate_ref), (up_hbm, up_ref), (grad_hbm, grad_ref)], sems)
    marks = slot_marks(chosen_ref[...], sources, cap, tokens)
    rows = contract(marks, arrived_ref[...], ((0,), (0,))).astype(jnp.bfloat16)
    pick = (iota((width, width), 0) == order_ref[...]).astype(jnp.float32).astype(jnp.bfloat16)
    ordered = jnp.dot(rows, pick, preferred_element_type=jnp.float32).astype(jnp.bfloat16)
    mine_ref[...] = ordered[:, :half]
    send_ref[:, :half] = ordered[:, half:]
    gate_in.wait()
    gate = jnp.dot(rows, gate_ref[...], preferred_element_type=jnp.float32)
    up_in.wait()
    up = jnp.dot(rows, up_ref[...], preferred_element_type=jnp.float32)
    squash = jax.nn.sigmoid(gate)
    grad_in.wait()
    upstream = grad_ref[...].astype(jnp.float32)
    send_ref[:, half : half + ff] = (upstream * up * (squash * (1.0 + gate * (1.0 - squash)))).astype(jnp.bfloat16)
    send_ref[:, half + ff :] = (upstream * (gate * squash)).astype(jnp.bfloat16)


def slot_grad_kernel(half, send_ref, gate_hbm, up_hbm, out_ref, gate_ref, up_ref, sems):
    ff = gate_ref.shape[1]
    gate_in, up_in = fetch([(gate_hbm, gate_ref), (up_hbm, up_ref)], sems)
    gate_in.wait()
    grad = contract(send_ref[:, half : half + ff], gate_ref[...], ((1,), (1,)))
    up_in.wait()
    grad = grad + contract(send_ref[:, half + ff :], up_ref[...], ((1,), (1,)))
    out_ref[...] = grad.astype(jnp.bfloat16)


def back_kernel(sources, cap, tokens, chosen_ref, grad_ref, after_ref, out_ref, stage_ref, sems):
    del after_ref
    marks = slot_marks(chosen_ref[...], sources, cap, tokens)
    marked_rows(marks, grad_ref[...], out_ref, stage_ref, sems)


def weight_kernel(mine_ref, send_ref, got_ref, after_ref, keep_ref, next_ref, past_ref, far_ref):
    del after_ref
    half = mine_ref.shape[1]
    block = half // FAN

    def part(q):
        cols = slice(q * block, (q + 1) * block)
        own = contract(mine_ref[:, cols], send_ref[:, half:], ((0,), (0,)))
        return own + contract(got_ref[:, cols], got_ref[:, half:], ((0,), (0,)))

    far_ref[...] = part(2).astype(jnp.bfloat16)
    next_ref[...] = part(1).astype(jnp.bfloat16)
    past_ref[...] = part(3).astype(jnp.bfloat16)
    keep_ref[...] = part(0)


def fold_kernel(rows, core_ref, keep_ref, next_hbm, far_hbm, past_hbm, out_ref, next_ref, far_ref, past_ref, sems):
    for copy in fetch([(next_hbm, next_ref), (far_hbm, far_ref), (past_hbm, past_ref)], sems):
        copy.wait()
    n = keep_ref.shape[0] // rows
    for a in range(n):
        here, before = pl.ds(a * rows, rows), pl.ds((a - 1 if a else n - 1) * rows, rows)
        total = next_ref[here].astype(jnp.float32) + far_ref[here].astype(jnp.float32)
        if a:
            total = total + keep_ref[before] + past_ref[before].astype(jnp.float32)
        else:
            total = total + jnp.where(core_ref[0] == 1, keep_ref[before], 0.0)
        out_ref[here] = total


def call(kernel, outs, *args, ins=None, out_space=None, scratch=(), mib=40):
    shapes = [jax.ShapeDtypeStruct(*o) for o in outs]
    spaces = [s or pltpu.VMEM for s in (ins or [None] * len(args))]
    out_specs = [pl.BlockSpec(memory_space=out_space or pltpu.VMEM) for _ in shapes]
    return pl.pallas_call(
        kernel,
        in_specs=[pl.BlockSpec(memory_space=s) for s in spaces],
        out_specs=out_specs if len(shapes) > 1 else out_specs[0],
        out_shape=shapes if len(shapes) > 1 else shapes[0],
        scratch_shapes=list(scratch),
        compiler_params=pltpu.CompilerParams(vmem_limit_bytes=mib * 2**20),
    )(*args)


def on_device(tokens, gate_weight, up_weight, hidden_grad, chosen, routes, route_count):
    tok_dev, width = tokens.shape
    slots, ff = hidden_grad.shape[2:]
    peers = lax.axis_size("expert")
    groups = lax.axis_size("dp")
    cap = min(tok_dev, 2 * slots // peers)
    chips = groups // 2
    rows = width // groups
    half = width // 2
    bf16, f32 = jnp.bfloat16, jnp.float32
    place = lax.axis_index("dp")
    z, core = place // 2, place % 2

    def along(value, hops):
        pairs = [(d, ((d // 2 + (hops if d % 2 == 0 else -hops)) % chips) * 2 + d % 2) for d in range(groups)]
        return lax.ppermute(value, "dp", pairs)

    def swap(value):
        return lax.ppermute(value, "dp", [(d, d ^ 1) for d in range(groups)])

    n = chips // 2 // FAN
    routes_t = routes.T
    count = route_count[None, :]
    picked = chosen[0]
    gate, up = gate_weight[0], up_weight[0]
    hbm, vmem, dma = pltpu.HBM, pltpu.VMEM, pltpu.SemaphoreType.DMA
    padded = peers * cap

    outgoing = call(
        functools.partial(dispatch_kernel, peers, cap, slots),
        [((padded, width), bf16)],
        tokens, routes_t, count,
        ins=[hbm] * 3,
        out_space=hbm,
        scratch=[
            vmem(tokens.shape, bf16), vmem(routes_t.shape, jnp.int32), vmem(count.shape, jnp.int32),
            vmem((padded, width), bf16), dma((3,)), dma((BLOCKS,)),
        ],
        mib=61,
    )
    arrived = lax.all_to_all(
        outgoing.reshape(peers, cap, width), "expert", split_axis=0, concat_axis=0, tiled=True
    ).reshape(padded, width)

    m = jnp.arange(width, dtype=jnp.int32)
    block = half // FAN
    which, q, i = m // half, (m % half) // block, (m % block) // (2 * rows)
    to_core = jnp.where(which == 0, core, 1 - core)
    last = jnp.where(to_core == 0, chips // 2, 0)
    ahead = jnp.where(q > 0, FAN * i + q, jnp.where(i == n - 1, last, FAN * (i + 1)))
    owner = (z + jnp.where(to_core == 0, ahead, -ahead) + chips) % chips
    order = (owner * 2 * rows + m % (2 * rows))[None, :]
    mine, send = call(
        functools.partial(delta_kernel, peers, cap, tok_dev),
        [((slots, half), bf16), ((slots, half + 2 * ff), bf16)],
        arrived, picked, order, gate, up, hidden_grad[0, 0],
        ins=[None] * 3 + [hbm] * 3,
        scratch=[vmem(a.shape, bf16) for a in (gate, up, hidden_grad[0, 0])] + [dma((3,))],
        mib=50,
    )
    got = swap(send)
    slot_grad = call(
        functools.partial(slot_grad_kernel, half),
        [((slots, width), bf16)],
        send, gate, up,
        ins=[None] + [hbm] * 2,
        scratch=[vmem(gate.shape, bf16), vmem(up.shape, bf16), dma((2,))],
        mib=50,
    )
    keep, to_1, to_past, to_2 = call(
        weight_kernel,
        [((block, 2 * ff), f32)] + [((block, 2 * ff), bf16)] * 3,
        mine, send, got, slot_grad,
        ins=[None] * 3 + [pl.ANY],
        mib=40,
    )
    from_past, from_1, from_2 = along(to_past, -1), along(to_1, 1), along(to_2, 2)
    end = slice(block - 2 * rows, block)
    total = (from_past[end].astype(f32) + jnp.where(core == 0, keep[end], 0.0)).astype(bf16)
    terms = call(
        functools.partial(fold_kernel, 2 * rows),
        [((block, 2 * ff), f32)],
        core[None], keep, from_1, from_2, from_past,
        ins=[pltpu.SMEM, None] + [hbm] * 3,
        scratch=[vmem((block, 2 * ff), bf16)] * 3 + [dma((3,))],
        mib=56,
    ).reshape(n, 2 * rows, 2 * ff)
    back = call(
        functools.partial(back_kernel, peers, cap, tok_dev),
        [((padded, width), bf16)],
        picked, slot_grad, total,
        ins=[None] * 2 + [pl.ANY],
        out_space=hbm,
        scratch=[vmem((padded, width), bf16), dma((BLOCKS,))],
    )
    returned = lax.all_to_all(back.reshape(peers, cap, width), "expert", split_axis=0, concat_axis=0, tiled=True)
    for t in range(1, n + 1):
        total = along(total, FAN)
        if t == TIE:
            total, returned = lax.optimization_barrier((total, returned))
        total = total.astype(f32) + terms[n - t]
        total = total.astype(bf16) if t < n else total
    low, high = total[:rows], total[rows:]
    other = swap(jnp.where(core == 0, high, low).astype(bf16))
    summed = (jnp.where(core == 0, low, high) + other.astype(f32)) / jnp.sqrt(f32(groups * slots))

    token_grad = call(
        functools.partial(combine_kernel, peers, cap, slots),
        [((tok_dev, width), bf16)],
        returned.reshape(padded, width), routes_t, count,
    )
    return token_grad, summed[None, :, :ff], summed[None, :, ff:]


def solution(mesh):
    return jax.shard_map(
        on_device,
        mesh=mesh,
        in_specs=(
            P(("dp", "expert"), None),
            P("expert", None, None),
            P("expert", None, None),
            P("dp", "expert", None, None),
            P("dp", "expert", None),
            P(("dp", "expert"), None),
            P(("dp", "expert")),
        ),
        out_specs=(P(("dp", "expert"), None), P("expert", "dp", None), P("expert", "dp", None)),
        check_vma=False,
    )
```

```python
import functools

import jax
import jax.numpy as jnp
from jax import lax
from jax.experimental import pallas as pl
from jax.experimental.pallas import tpu as pltpu
from jax.sharding import PartitionSpec as P

FAN = 4
TIE = 3
BLOCKS = 4


def iota(shape, dim):
    return lax.broadcasted_iota(jnp.int32, shape, dim)


def place_rows(member, cap):
    n, m = member.shape
    ones = member.astype(jnp.float32).astype(jnp.bfloat16)
    before = (iota((m, m), 0) < iota((m, m), 1)).astype(jnp.float32).astype(jnp.bfloat16)
    rank = jnp.dot(ones, before, preferred_element_type=jnp.float32)
    rank = jnp.where(member, rank, -1.0).astype(jnp.int32)
    marks = rank[:, None, :] == iota((n, cap, m), 1)
    return marks.astype(jnp.float32).reshape(n * cap, m).astype(jnp.bfloat16)


def token_marks(routes, count, experts, cap, slots):
    depth, tokens = routes.shape
    rows = iota((experts, tokens), 0)
    member = jnp.zeros((experts, tokens), jnp.int32)
    for r in range(depth):
        owner = jnp.where(count > r, lax.div(routes[r : r + 1], jnp.int32(slots)), -1)
        member = member + (owner == rows).astype(jnp.int32)
    return place_rows(member > 0, cap)


def slot_marks(chosen, sources, cap, tokens):
    source = lax.div(chosen, jnp.int32(tokens))
    return place_rows(source == iota((sources, chosen.shape[1]), 0), cap)


def contract(a, b, dims):
    return lax.dot_general(a, b, (dims, ((), ())), preferred_element_type=jnp.float32)


def fetch(pairs, sems):
    copies = [pltpu.make_async_copy(src, dst, sems.at[i]) for i, (src, dst) in enumerate(pairs)]
    for copy in copies:
        copy.start()
    return copies


def marked_rows(marks, rows, out_ref, stage_ref, sems):
    size = marks.shape[0] // BLOCKS
    copies = []
    for i in range(BLOCKS):
        span = pl.ds(i * size, size)
        block = jnp.dot(marks[i * size : (i + 1) * size], rows, preferred_element_type=jnp.float32)
        stage_ref[span] = block.astype(jnp.bfloat16)
        copies.append(pltpu.make_async_copy(stage_ref.at[span], out_ref.at[span], sems.at[i]))
        copies[-1].start()
    for copy in copies:
        copy.wait()


def dispatch_kernel(experts, cap, slots, tokens_hbm, routes_hbm, count_hbm, out_ref, tokens_ref, routes_ref, count_ref, stage_ref, in_sems, out_sems):
    tokens_in, routes_in, count_in = fetch(
        [(tokens_hbm, tokens_ref), (routes_hbm, routes_ref), (count_hbm, count_ref)], in_sems
    )
    routes_in.wait()
    count_in.wait()
    marks = token_marks(routes_ref[...], count_ref[...], experts, cap, slots)
    tokens_in.wait()
    marked_rows(marks, tokens_ref[...], out_ref, stage_ref, out_sems)


def combine_kernel(experts, cap, slots, back_ref, routes_ref, count_ref, out_ref):
    marks = token_marks(routes_ref[...], count_ref[...], experts, cap, slots)
    out_ref[...] = contract(marks, back_ref[...], ((0,), (0,))).astype(jnp.bfloat16)


def delta_kernel(sources, cap, tokens, arrived_ref, chosen_ref, order_ref, gate_hbm, up_hbm, grad_hbm, mine_ref, send_ref, gate_ref, up_ref, grad_ref, sems):
    ff = gate_ref.shape[1]
    width = arrived_ref.shape[1]
    half = width // 2
    gate_in, up_in, grad_in = fetch([(gate_hbm, gate_ref), (up_hbm, up_ref), (grad_hbm, grad_ref)], sems)
    marks = slot_marks(chosen_ref[...], sources, cap, tokens)
    rows = contract(marks, arrived_ref[...], ((0,), (0,))).astype(jnp.bfloat16)
    pick = (iota((width, width), 0) == order_ref[...]).astype(jnp.float32).astype(jnp.bfloat16)
    ordered = jnp.dot(rows, pick, preferred_element_type=jnp.float32).astype(jnp.bfloat16)
    mine_ref[...] = ordered[:, :half]
    send_ref[:, :half] = ordered[:, half:]
    gate_in.wait()
    gate = jnp.dot(rows, gate_ref[...], preferred_element_type=jnp.float32)
    up_in.wait()
    up = jnp.dot(rows, up_ref[...], preferred_element_type=jnp.float32)
    squash = jax.nn.sigmoid(gate)
    grad_in.wait()
    upstream = grad_ref[...].astype(jnp.float32)
    send_ref[:, half : half + ff] = (upstream * up * (squash * (1.0 + gate * (1.0 - squash)))).astype(jnp.bfloat16)
    send_ref[:, half + ff :] = (upstream * (gate * squash)).astype(jnp.bfloat16)


def slot_grad_kernel(half, send_ref, gate_hbm, up_hbm, out_ref, gate_ref, up_ref, sems):
    ff = gate_ref.shape[1]
    gate_in, up_in = fetch([(gate_hbm, gate_ref), (up_hbm, up_ref)], sems)
    gate_in.wait()
    grad = contract(send_ref[:, half : half + ff], gate_ref[...], ((1,), (1,)))
    up_in.wait()
    grad = grad + contract(send_ref[:, half + ff :], up_ref[...], ((1,), (1,)))
    out_ref[...] = grad.astype(jnp.bfloat16)


def back_kernel(sources, cap, tokens, chosen_ref, grad_ref, after_ref, out_ref, stage_ref, sems):
    del after_ref
    marks = slot_marks(chosen_ref[...], sources, cap, tokens)
    marked_rows(marks, grad_ref[...], out_ref, stage_ref, sems)


def weight_kernel(mine_ref, send_ref, got_ref, after_ref, keep_ref, next_ref, past_ref, far_ref):
    del after_ref
    half = mine_ref.shape[1]
    block = half // FAN

    def part(q):
        cols = slice(q * block, (q + 1) * block)
        own = contract(mine_ref[:, cols], send_ref[:, half:], ((0,), (0,)))
        return own + contract(got_ref[:, cols], got_ref[:, half:], ((0,), (0,)))

    far_ref[...] = part(2).astype(jnp.bfloat16)
    next_ref[...] = part(1).astype(jnp.bfloat16)
    past_ref[...] = part(3).astype(jnp.bfloat16)
    keep_ref[...] = part(0)


def call(kernel, outs, *args, ins=None, out_space=None, scratch=(), mib=40):
    shapes = [jax.ShapeDtypeStruct(*o) for o in outs]
    spaces = [s or pltpu.VMEM for s in (ins or [None] * len(args))]
    out_specs = [pl.BlockSpec(memory_space=out_space or pltpu.VMEM) for _ in shapes]
    return pl.pallas_call(
        kernel,
        in_specs=[pl.BlockSpec(memory_space=s) for s in spaces],
        out_specs=out_specs if len(shapes) > 1 else out_specs[0],
        out_shape=shapes if len(shapes) > 1 else shapes[0],
        scratch_shapes=list(scratch),
        compiler_params=pltpu.CompilerParams(vmem_limit_bytes=mib * 2**20),
    )(*args)


def on_device(tokens, gate_weight, up_weight, hidden_grad, chosen, routes, route_count):
    tok_dev, width = tokens.shape
    slots, ff = hidden_grad.shape[2:]
    peers = lax.axis_size("expert")
    groups = lax.axis_size("dp")
    cap = min(tok_dev, 2 * slots // peers)
    chips = groups // 2
    rows = width // groups
    half = width // 2
    bf16, f32 = jnp.bfloat16, jnp.float32
    place = lax.axis_index("dp")
    z, core = place // 2, place % 2

    def along(value, hops):
        pairs = [(d, ((d // 2 + (hops if d % 2 == 0 else -hops)) % chips) * 2 + d % 2) for d in range(groups)]
        return lax.ppermute(value, "dp", pairs)

    def swap(value):
        return lax.ppermute(value, "dp", [(d, d ^ 1) for d in range(groups)])

    n = chips // 2 // FAN
    routes_t = routes.T
    count = route_count[None, :]
    picked = chosen[0]
    gate, up = gate_weight[0], up_weight[0]
    hbm, vmem, dma = pltpu.HBM, pltpu.VMEM, pltpu.SemaphoreType.DMA
    padded = peers * cap

    outgoing = call(
        functools.partial(dispatch_kernel, peers, cap, slots),
        [((padded, width), bf16)],
        tokens, routes_t, count,
        ins=[hbm] * 3,
        out_space=hbm,
        scratch=[
            vmem(tokens.shape, bf16), vmem(routes_t.shape, jnp.int32), vmem(count.shape, jnp.int32),
            vmem((padded, width), bf16), dma((3,)), dma((BLOCKS,)),
        ],
        mib=61,
    )
    arrived = lax.all_to_all(
        outgoing.reshape(peers, cap, width), "expert", split_axis=0, concat_axis=0, tiled=True
    ).reshape(padded, width)

    m = jnp.arange(width, dtype=jnp.int32)
    block = half // FAN
    which, q, i = m // half, (m % half) // block, (m % block) // (2 * rows)
    to_core = jnp.where(which == 0, core, 1 - core)
    last = jnp.where(to_core == 0, chips // 2, 0)
    ahead = jnp.where(q > 0, FAN * i + q, jnp.where(i == n - 1, last, FAN * (i + 1)))
    owner = (z + jnp.where(to_core == 0, ahead, -ahead) + chips) % chips
    order = (owner * 2 * rows + m % (2 * rows))[None, :]
    mine, send = call(
        functools.partial(delta_kernel, peers, cap, tok_dev),
        [((slots, half), bf16), ((slots, half + 2 * ff), bf16)],
        arrived, picked, order, gate, up, hidden_grad[0, 0],
        ins=[None] * 3 + [hbm] * 3,
        scratch=[vmem(a.shape, bf16) for a in (gate, up, hidden_grad[0, 0])] + [dma((3,))],
        mib=50,
    )
    got = swap(send)
    slot_grad = call(
        functools.partial(slot_grad_kernel, half),
        [((slots, width), bf16)],
        send, gate, up,
        ins=[None] + [hbm] * 2,
        scratch=[vmem(gate.shape, bf16), vmem(up.shape, bf16), dma((2,))],
        mib=50,
    )
    keep, to_1, to_past, to_2 = call(
        weight_kernel,
        [((block, 2 * ff), f32)] + [((block, 2 * ff), bf16)] * 3,
        mine, send, got, slot_grad,
        ins=[None] * 3 + [pl.ANY],
        mib=40,
    )
    from_past, from_1, from_2 = along(to_past, -1), along(to_1, 1), along(to_2, 2)
    end = slice(block - 2 * rows, block)
    total = (from_past[end].astype(f32) + jnp.where(core == 0, keep[end], 0.0)).astype(bf16)
    before = [keep[a * 2 * rows : (a + 1) * 2 * rows] for a in range(n)]
    terms = jnp.concatenate([jnp.where(core == 1, before[-1], 0.0)] + before[:-1])
    behind = jnp.concatenate([jnp.zeros_like(from_past[: 2 * rows]), from_past[: block - 2 * rows]])
    terms = terms + from_1.astype(f32) + from_2.astype(f32) + behind.astype(f32)
    terms = lax.optimization_barrier(terms).reshape(n, 2 * rows, 2 * ff)
    back = call(
        functools.partial(back_kernel, peers, cap, tok_dev),
        [((padded, width), bf16)],
        picked, slot_grad, total,
        ins=[None] * 2 + [pl.ANY],
        out_space=hbm,
        scratch=[vmem((padded, width), bf16), dma((BLOCKS,))],
    )
    returned = lax.all_to_all(back.reshape(peers, cap, width), "expert", split_axis=0, concat_axis=0, tiled=True)
    for t in range(1, n + 1):
        total = along(total, FAN)
        if t == TIE:
            total, returned = lax.optimization_barrier((total, returned))
        total = total.astype(f32) + terms[n - t]
        total = total.astype(bf16) if t < n else total
    low, high = total[:rows], total[rows:]
    other = swap(jnp.where(core == 0, high, low).astype(bf16))
    summed = (jnp.where(core == 0, low, high) + other.astype(f32)) / jnp.sqrt(f32(groups * slots))

    token_grad = call(
        functools.partial(combine_kernel, peers, cap, slots),
        [((tok_dev, width), bf16)],
        returned.reshape(padded, width), routes_t, count,
    )
    return token_grad, summed[None, :, :ff], summed[None, :, ff:]


def solution(mesh):
    return jax.shard_map(
        on_device,
        mesh=mesh,
        in_specs=(
            P(("dp", "expert"), None),
            P("expert", None, None),
            P("expert", None, None),
            P("dp", "expert", None, None),
            P("dp", "expert", None),
            P(("dp", "expert"), None),
            P(("dp", "expert")),
        ),
        out_specs=(P(("dp", "expert"), None), P("expert", "dp", None), P("expert", "dp", None)),
        check_vma=False,
    )
```

```python
import functools

import jax
import jax.numpy as jnp
from jax import lax
from jax.experimental import pallas as pl
from jax.experimental.pallas import tpu as pltpu
from jax.sharding import PartitionSpec as P

FAN = 4
TIE = 3
BLOCKS = 4


def iota(shape, dim):
    return lax.broadcasted_iota(jnp.int32, shape, dim)


def place_rows(member, cap):
    n, m = member.shape
    ones = member.astype(jnp.float32).astype(jnp.bfloat16)
    before = (iota((m, m), 0) < iota((m, m), 1)).astype(jnp.float32).astype(jnp.bfloat16)
    rank = jnp.dot(ones, before, preferred_element_type=jnp.float32)
    rank = jnp.where(member, rank, -1.0).astype(jnp.int32)
    marks = rank[:, None, :] == iota((n, cap, m), 1)
    return marks.astype(jnp.float32).reshape(n * cap, m).astype(jnp.bfloat16)


def token_marks(routes, count, experts, cap, slots):
    depth, tokens = routes.shape
    rows = iota((experts, tokens), 0)
    member = jnp.zeros((experts, tokens), jnp.int32)
    for r in range(depth):
        owner = jnp.where(count > r, lax.div(routes[r : r + 1], jnp.int32(slots)), -1)
        member = member + (owner == rows).astype(jnp.int32)
    return place_rows(member > 0, cap)


def slot_marks(chosen, sources, cap, tokens):
    source = lax.div(chosen, jnp.int32(tokens))
    return place_rows(source == iota((sources, chosen.shape[1]), 0), cap)


def contract(a, b, dims):
    return lax.dot_general(a, b, (dims, ((), ())), preferred_element_type=jnp.float32)


def fetch(pairs, sems):
    copies = [pltpu.make_async_copy(src, dst, sems.at[i]) for i, (src, dst) in enumerate(pairs)]
    for copy in copies:
        copy.start()
    return copies


def marked_rows(marks, rows, out_ref, stage_ref, sems):
    size = marks.shape[0] // BLOCKS
    copies = []
    for i in range(BLOCKS):
        span = pl.ds(i * size, size)
        block = jnp.dot(marks[i * size : (i + 1) * size], rows, preferred_element_type=jnp.float32)
        stage_ref[span] = block.astype(jnp.bfloat16)
        copies.append(pltpu.make_async_copy(stage_ref.at[span], out_ref.at[span], sems.at[i]))
        copies[-1].start()
    for copy in copies:
        copy.wait()


def dispatch_kernel(experts, cap, slots, tokens_hbm, routes_hbm, count_hbm, out_ref, tokens_ref, routes_ref, count_ref, stage_ref, in_sems, out_sems):
    tokens_in, routes_in, count_in = fetch(
        [(tokens_hbm, tokens_ref), (routes_hbm, routes_ref), (count_hbm, count_ref)], in_sems
    )
    routes_in.wait()
    count_in.wait()
    marks = token_marks(routes_ref[...], count_ref[...], experts, cap, slots)
    tokens_in.wait()
    marked_rows(marks, tokens_ref[...], out_ref, stage_ref, out_sems)


def combine_kernel(experts, cap, slots, back_ref, routes_ref, count_ref, out_ref):
    marks = token_marks(routes_ref[...], count_ref[...], experts, cap, slots)
    out_ref[...] = contract(marks, back_ref[...], ((0,), (0,))).astype(jnp.bfloat16)


def delta_kernel(sources, cap, tokens, arrived_ref, chosen_ref, order_ref, gate_hbm, up_hbm, grad_hbm, mine_ref, send_ref, gate_ref, up_ref, grad_ref, sems):
    ff = gate_ref.shape[1]
    width = arrived_ref.shape[1]
    half = width // 2
    gate_in, up_in, grad_in = fetch([(gate_hbm, gate_ref), (up_hbm, up_ref), (grad_hbm, grad_ref)], sems)
    marks = slot_marks(chosen_ref[...], sources, cap, tokens)
    rows = contract(marks, arrived_ref[...], ((0,), (0,))).astype(jnp.bfloat16)
    pick = (iota((width, width), 0) == order_ref[...]).astype(jnp.float32).astype(jnp.bfloat16)
    ordered = jnp.dot(rows, pick, preferred_element_type=jnp.float32).astype(jnp.bfloat16)
    mine_ref[...] = ordered[:, :half]
    send_ref[:, :half] = ordered[:, half:]
    gate_in.wait()
    gate = jnp.dot(rows, gate_ref[...], preferred_element_type=jnp.float32)
    up_in.wait()
    up = jnp.dot(rows, up_ref[...], preferred_element_type=jnp.float32)
    squash = jax.nn.sigmoid(gate)
    grad_in.wait()
    upstream = grad_ref[...].astype(jnp.float32)
    send_ref[:, half : half + ff] = (upstream * up * (squash * (1.0 + gate * (1.0 - squash)))).astype(jnp.bfloat16)
    send_ref[:, half + ff :] = (upstream * (gate * squash)).astype(jnp.bfloat16)


def slot_grad_kernel(half, send_ref, gate_hbm, up_hbm, out_ref, gate_ref, up_ref, sems):
    ff = gate_ref.shape[1]
    gate_in, up_in = fetch([(gate_hbm, gate_ref), (up_hbm, up_ref)], sems)
    gate_in.wait()
    grad = contract(send_ref[:, half : half + ff], gate_ref[...], ((1,), (1,)))
    up_in.wait()
    grad = grad + contract(send_ref[:, half + ff :], up_ref[...], ((1,), (1,)))
    out_ref[...] = grad.astype(jnp.bfloat16)


def back_kernel(sources, cap, tokens, chosen_ref, grad_ref, after_ref, out_ref, stage_ref, sems):
    del after_ref
    marks = slot_marks(chosen_ref[...], sources, cap, tokens)
    marked_rows(marks, grad_ref[...], out_ref, stage_ref, sems)


def weight_kernel(mine_ref, send_ref, got_ref, after_ref, keep_ref, next_ref, past_ref, far_ref):
    del after_ref
    half = mine_ref.shape[1]
    block = half // FAN

    def part(q):
        cols = slice(q * block, (q + 1) * block)
        own = contract(mine_ref[:, cols], send_ref[:, half:], ((0,), (0,)))
        return own + contract(got_ref[:, cols], got_ref[:, half:], ((0,), (0,)))

    far_ref[...] = part(2).astype(jnp.bfloat16)
    next_ref[...] = part(1).astype(jnp.bfloat16)
    past_ref[...] = part(3).astype(jnp.bfloat16)
    keep_ref[...] = part(0)


def call(kernel, outs, *args, ins=None, out_space=None, scratch=(), mib=40):
    shapes = [jax.ShapeDtypeStruct(*o) for o in outs]
    spaces = [s or pltpu.VMEM for s in (ins or [None] * len(args))]
    out_specs = [pl.BlockSpec(memory_space=out_space or pltpu.VMEM) for _ in shapes]
    return pl.pallas_call(
        kernel,
        in_specs=[pl.BlockSpec(memory_space=s) for s in spaces],
        out_specs=out_specs if len(shapes) > 1 else out_specs[0],
        out_shape=shapes if len(shapes) > 1 else shapes[0],
        scratch_shapes=list(scratch),
        compiler_params=pltpu.CompilerParams(vmem_limit_bytes=mib * 2**20),
    )(*args)


def on_device(tokens, gate_weight, up_weight, hidden_grad, chosen, routes, route_count):
    tok_dev, width = tokens.shape
    slots, ff = hidden_grad.shape[2:]
    peers = lax.axis_size("expert")
    groups = lax.axis_size("dp")
    cap = min(tok_dev, 2 * slots // peers)
    chips = groups // 2
    rows = width // groups
    half = width // 2
    bf16, f32 = jnp.bfloat16, jnp.float32
    place = lax.axis_index("dp")
    z, core = place // 2, place % 2

    def along(value, hops):
        pairs = [(d, ((d // 2 + (hops if d % 2 == 0 else -hops)) % chips) * 2 + d % 2) for d in range(groups)]
        return lax.ppermute(value, "dp", pairs)

    def swap(value):
        return lax.ppermute(value, "dp", [(d, d ^ 1) for d in range(groups)])

    n = chips // 2 // FAN
    routes_t = routes.T
    count = route_count[None, :]
    picked = chosen[0]
    gate, up = gate_weight[0], up_weight[0]
    hbm, vmem, dma = pltpu.HBM, pltpu.VMEM, pltpu.SemaphoreType.DMA
    padded = peers * cap

    outgoing = call(
        functools.partial(dispatch_kernel, peers, cap, slots),
        [((padded, width), bf16)],
        tokens, routes_t, count,
        ins=[hbm] * 3,
        out_space=hbm,
        scratch=[
            vmem(tokens.shape, bf16), vmem(routes_t.shape, jnp.int32), vmem(count.shape, jnp.int32),
            vmem((padded, width), bf16), dma((3,)), dma((BLOCKS,)),
        ],
        mib=61,
    )
    arrived = lax.all_to_all(
        outgoing.reshape(peers, cap, width), "expert", split_axis=0, concat_axis=0, tiled=True
    ).reshape(padded, width)

    m = jnp.arange(width, dtype=jnp.int32)
    block = half // FAN
    which, q, i = m // half, (m % half) // block, (m % block) // (2 * rows)
    to_core = jnp.where(which == 0, core, 1 - core)
    first = jnp.where(q == 0, jnp.where(to_core == 0, chips // 2, 0), chips // 2 - 1)
    ahead = jnp.where((q == 1) | (q == 2), FAN * i + q, jnp.where(i == 0, first, FAN * i - jnp.where(q == 0, 0, 1)))
    owner = (z + jnp.where(to_core == 0, ahead, -ahead) + chips) % chips
    order = (owner * 2 * rows + m % (2 * rows))[None, :]
    mine, send = call(
        functools.partial(delta_kernel, peers, cap, tok_dev),
        [((slots, half), bf16), ((slots, half + 2 * ff), bf16)],
        arrived, picked, order, gate, up, hidden_grad[0, 0],
        ins=[None] * 3 + [hbm] * 3,
        scratch=[vmem(a.shape, bf16) for a in (gate, up, hidden_grad[0, 0])] + [dma((3,))],
        mib=50,
    )
    got = swap(send)
    slot_grad = call(
        functools.partial(slot_grad_kernel, half),
        [((slots, width), bf16)],
        send, gate, up,
        ins=[None] + [hbm] * 2,
        scratch=[vmem(gate.shape, bf16), vmem(up.shape, bf16), dma((2,))],
        mib=50,
    )
    keep, to_1, to_past, to_2 = call(
        weight_kernel,
        [((block, 2 * ff), f32)] + [((block, 2 * ff), bf16)] * 3,
        mine, send, got, slot_grad,
        ins=[None] * 3 + [pl.ANY],
        mib=40,
    )
    from_past, from_1, from_2 = along(to_past, -1), along(to_1, 1), along(to_2, 2)
    piece = 2 * rows
    total = (from_past[:piece].astype(f32) + jnp.where(core == 0, keep[:piece], 0.0)).astype(bf16)
    inner = jnp.arange(block)[:, None] >= piece
    terms = jnp.where(inner, keep + from_past.astype(f32), jnp.where(core == 1, keep, 0.0))
    terms = terms + from_1.astype(f32) + from_2.astype(f32)
    terms = lax.optimization_barrier(terms).reshape(n, piece, 2 * ff)
    back = call(
        functools.partial(back_kernel, peers, cap, tok_dev),
        [((padded, width), bf16)],
        picked, slot_grad, total,
        ins=[None] * 2 + [pl.ANY],
        out_space=hbm,
        scratch=[vmem((padded, width), bf16), dma((BLOCKS,))],
    )
    returned = lax.all_to_all(back.reshape(peers, cap, width), "expert", split_axis=0, concat_axis=0, tiled=True)
    for t in range(1, n + 1):
        total = along(total, FAN)
        if t == TIE:
            total, returned = lax.optimization_barrier((total, returned))
        total = total.astype(f32) + terms[n - t]
        total = total.astype(bf16) if t < n else total
    low, high = total[:rows], total[rows:]
    other = swap(jnp.where(core == 0, high, low).astype(bf16))
    summed = (jnp.where(core == 0, low, high) + other.astype(f32)) / jnp.sqrt(f32(groups * slots))

    token_grad = call(
        functools.partial(combine_kernel, peers, cap, slots),
        [((tok_dev, width), bf16)],
        returned.reshape(padded, width), routes_t, count,
    )
    return token_grad, summed[None, :, :ff], summed[None, :, ff:]


def solution(mesh):
    return jax.shard_map(
        on_device,
        mesh=mesh,
        in_specs=(
            P(("dp", "expert"), None),
            P("expert", None, None),
            P("expert", None, None),
            P("dp", "expert", None, None),
            P("dp", "expert", None),
            P(("dp", "expert"), None),
            P(("dp", "expert")),
        ),
        out_specs=(P(("dp", "expert"), None), P("expert", "dp", None), P("expert", "dp", None)),
        check_vma=False,
    )
```

```python
import functools

import jax
import jax.numpy as jnp
from jax import lax
from jax.experimental import pallas as pl
from jax.experimental.pallas import tpu as pltpu
from jax.sharding import PartitionSpec as P

FAN = 4
TIE = 4
BLOCKS = 4


def iota(shape, dim):
    return lax.broadcasted_iota(jnp.int32, shape, dim)


def place_rows(member, cap):
    n, m = member.shape
    ones = member.astype(jnp.float32).astype(jnp.bfloat16)
    before = (iota((m, m), 0) < iota((m, m), 1)).astype(jnp.float32).astype(jnp.bfloat16)
    rank = jnp.dot(ones, before, preferred_element_type=jnp.float32)
    rank = jnp.where(member, rank, -1.0).astype(jnp.int32)
    marks = rank[:, None, :] == iota((n, cap, m), 1)
    return marks.astype(jnp.float32).reshape(n * cap, m).astype(jnp.bfloat16)


def token_marks(routes, count, experts, cap, slots):
    depth, tokens = routes.shape
    rows = iota((experts, tokens), 0)
    member = jnp.zeros((experts, tokens), jnp.int32)
    for r in range(depth):
        owner = jnp.where(count > r, lax.div(routes[r : r + 1], jnp.int32(slots)), -1)
        member = member + (owner == rows).astype(jnp.int32)
    return place_rows(member > 0, cap)


def slot_marks(chosen, sources, cap, tokens):
    source = lax.div(chosen, jnp.int32(tokens))
    return place_rows(source == iota((sources, chosen.shape[1]), 0), cap)


def contract(a, b, dims):
    return lax.dot_general(a, b, (dims, ((), ())), preferred_element_type=jnp.float32)


def fetch(pairs, sems):
    copies = [pltpu.make_async_copy(src, dst, sems.at[i]) for i, (src, dst) in enumerate(pairs)]
    for copy in copies:
        copy.start()
    return copies


def marked_rows(marks, rows, out_ref, stage_ref, sems):
    size = marks.shape[0] // BLOCKS
    copies = []
    for i in range(BLOCKS):
        span = pl.ds(i * size, size)
        block = jnp.dot(marks[i * size : (i + 1) * size], rows, preferred_element_type=jnp.float32)
        stage_ref[span] = block.astype(jnp.bfloat16)
        copies.append(pltpu.make_async_copy(stage_ref.at[span], out_ref.at[span], sems.at[i]))
        copies[-1].start()
    for copy in copies:
        copy.wait()


def dispatch_kernel(experts, cap, slots, tokens_hbm, routes_hbm, count_hbm, out_ref, tokens_ref, routes_ref, count_ref, stage_ref, in_sems, out_sems):
    tokens_in, routes_in, count_in = fetch(
        [(tokens_hbm, tokens_ref), (routes_hbm, routes_ref), (count_hbm, count_ref)], in_sems
    )
    routes_in.wait()
    count_in.wait()
    marks = token_marks(routes_ref[...], count_ref[...], experts, cap, slots)
    tokens_in.wait()
    marked_rows(marks, tokens_ref[...], out_ref, stage_ref, out_sems)


def combine_kernel(experts, cap, slots, back_ref, routes_ref, count_ref, out_ref):
    marks = token_marks(routes_ref[...], count_ref[...], experts, cap, slots)
    out_ref[...] = contract(marks, back_ref[...], ((0,), (0,))).astype(jnp.bfloat16)


def delta_kernel(sources, cap, tokens, arrived_ref, chosen_ref, order_ref, gate_hbm, up_hbm, grad_hbm, mine_ref, send_ref, gate_ref, up_ref, grad_ref, sems):
    ff = gate_ref.shape[1]
    width = arrived_ref.shape[1]
    half = width // 2
    gate_in, up_in, grad_in = fetch([(gate_hbm, gate_ref), (up_hbm, up_ref), (grad_hbm, grad_ref)], sems)
    marks = slot_marks(chosen_ref[...], sources, cap, tokens)
    rows = contract(marks, arrived_ref[...], ((0,), (0,))).astype(jnp.bfloat16)
    pick = (iota((width, width), 0) == order_ref[...]).astype(jnp.float32).astype(jnp.bfloat16)
    ordered = jnp.dot(rows, pick, preferred_element_type=jnp.float32).astype(jnp.bfloat16)
    mine_ref[...] = ordered[:, :half]
    send_ref[:, :half] = ordered[:, half:]
    gate_in.wait()
    gate = jnp.dot(rows, gate_ref[...], preferred_element_type=jnp.float32)
    up_in.wait()
    up = jnp.dot(rows, up_ref[...], preferred_element_type=jnp.float32)
    squash = jax.nn.sigmoid(gate)
    grad_in.wait()
    upstream = grad_ref[...].astype(jnp.float32)
    send_ref[:, half : half + ff] = (upstream * up * (squash * (1.0 + gate * (1.0 - squash)))).astype(jnp.bfloat16)
    send_ref[:, half + ff :] = (upstream * (gate * squash)).astype(jnp.bfloat16)


def slot_grad_kernel(half, send_ref, gate_hbm, up_hbm, out_ref, gate_ref, up_ref, sems):
    ff = gate_ref.shape[1]
    gate_in, up_in = fetch([(gate_hbm, gate_ref), (up_hbm, up_ref)], sems)
    gate_in.wait()
    grad = contract(send_ref[:, half : half + ff], gate_ref[...], ((1,), (1,)))
    up_in.wait()
    grad = grad + contract(send_ref[:, half + ff :], up_ref[...], ((1,), (1,)))
    out_ref[...] = grad.astype(jnp.bfloat16)


def back_kernel(sources, cap, tokens, chosen_ref, grad_ref, after_ref, out_ref, stage_ref, sems):
    del after_ref
    marks = slot_marks(chosen_ref[...], sources, cap, tokens)
    marked_rows(marks, grad_ref[...], out_ref, stage_ref, sems)


def weight_kernel(mine_ref, send_ref, got_ref, after_ref, keep_ref, next_ref, past_ref, far_ref):
    del after_ref
    half = mine_ref.shape[1]
    block = half // FAN

    def part(q):
        cols = slice(q * block, (q + 1) * block)
        own = contract(mine_ref[:, cols], send_ref[:, half:], ((0,), (0,)))
        return own + contract(got_ref[:, cols], got_ref[:, half:], ((0,), (0,)))

    far_ref[...] = part(2).astype(jnp.bfloat16)
    next_ref[...] = part(1).astype(jnp.bfloat16)
    past_ref[...] = part(3).astype(jnp.bfloat16)
    keep_ref[...] = part(0)


def call(kernel, outs, *args, ins=None, out_space=None, scratch=(), mib=40):
    shapes = [jax.ShapeDtypeStruct(*o) for o in outs]
    spaces = [s or pltpu.VMEM for s in (ins or [None] * len(args))]
    out_specs = [pl.BlockSpec(memory_space=out_space or pltpu.VMEM) for _ in shapes]
    return pl.pallas_call(
        kernel,
        in_specs=[pl.BlockSpec(memory_space=s) for s in spaces],
        out_specs=out_specs if len(shapes) > 1 else out_specs[0],
        out_shape=shapes if len(shapes) > 1 else shapes[0],
        scratch_shapes=list(scratch),
        compiler_params=pltpu.CompilerParams(vmem_limit_bytes=mib * 2**20),
    )(*args)


def on_device(tokens, gate_weight, up_weight, hidden_grad, chosen, routes, route_count):
    tok_dev, width = tokens.shape
    slots, ff = hidden_grad.shape[2:]
    peers = lax.axis_size("expert")
    groups = lax.axis_size("dp")
    cap = min(tok_dev, 2 * slots // peers)
    chips = groups // 2
    rows = width // groups
    half = width // 2
    bf16, f32 = jnp.bfloat16, jnp.float32
    place = lax.axis_index("dp")
    z, core = place // 2, place % 2

    def along(value, hops):
        pairs = [(d, ((d // 2 + (hops if d % 2 == 0 else -hops)) % chips) * 2 + d % 2) for d in range(groups)]
        return lax.ppermute(value, "dp", pairs)

    def swap(value):
        return lax.ppermute(value, "dp", [(d, d ^ 1) for d in range(groups)])

    n = chips // 2 // FAN
    routes_t = routes.T
    count = route_count[None, :]
    picked = chosen[0]
    gate, up = gate_weight[0], up_weight[0]
    hbm, vmem, dma = pltpu.HBM, pltpu.VMEM, pltpu.SemaphoreType.DMA
    padded = peers * cap

    outgoing = call(
        functools.partial(dispatch_kernel, peers, cap, slots),
        [((padded, width), bf16)],
        tokens, routes_t, count,
        ins=[hbm] * 3,
        out_space=hbm,
        scratch=[
            vmem(tokens.shape, bf16), vmem(routes_t.shape, jnp.int32), vmem(count.shape, jnp.int32),
            vmem((padded, width), bf16), dma((3,)), dma((BLOCKS,)),
        ],
        mib=61,
    )
    arrived = lax.all_to_all(
        outgoing.reshape(peers, cap, width), "expert", split_axis=0, concat_axis=0, tiled=True
    ).reshape(padded, width)

    m = jnp.arange(width, dtype=jnp.int32)
    block = half // FAN
    which, q, i = m // half, (m % half) // block, (m % block) // (2 * rows)
    to_core = jnp.where(which == 0, core, 1 - core)
    first = jnp.where(q == 0, jnp.where(to_core == 0, chips // 2, 0), chips // 2 - 1)
    ahead = jnp.where((q == 1) | (q == 2), FAN * i + q, jnp.where(i == 0, first, FAN * i - jnp.where(q == 0, 0, 1)))
    owner = (z + jnp.where(to_core == 0, ahead, -ahead) + chips) % chips
    order = (owner * 2 * rows + m % (2 * rows))[None, :]
    mine, send = call(
        functools.partial(delta_kernel, peers, cap, tok_dev),
        [((slots, half), bf16), ((slots, half + 2 * ff), bf16)],
        arrived, picked, order, gate, up, hidden_grad[0, 0],
        ins=[None] * 3 + [hbm] * 3,
        scratch=[vmem(a.shape, bf16) for a in (gate, up, hidden_grad[0, 0])] + [dma((3,))],
        mib=50,
    )
    got = swap(send)
    slot_grad = call(
        functools.partial(slot_grad_kernel, half),
        [((slots, width), bf16)],
        send, gate, up,
        ins=[None] + [hbm] * 2,
        scratch=[vmem(gate.shape, bf16), vmem(up.shape, bf16), dma((2,))],
        mib=50,
    )
    keep, to_1, to_past, to_2 = call(
        weight_kernel,
        [((block, 2 * ff), f32)] + [((block, 2 * ff), bf16)] * 3,
        mine, send, got, slot_grad,
        ins=[None] * 3 + [pl.ANY],
        mib=40,
    )
    from_past, from_1, from_2 = along(to_past, -1), along(to_1, 1), along(to_2, 2)
    piece = 2 * rows
    total = (from_past[:piece].astype(f32) + jnp.where(core == 0, keep[:piece], 0.0)).astype(bf16)
    inner = jnp.arange(block)[:, None] >= piece
    terms = jnp.where(inner, keep + from_past.astype(f32), jnp.where(core == 1, keep, 0.0))
    terms = terms + from_1.astype(f32) + from_2.astype(f32)
    terms = lax.optimization_barrier(terms).reshape(n, piece, 2 * ff)
    back = call(
        functools.partial(back_kernel, peers, cap, tok_dev),
        [((padded, width), bf16)],
        picked, slot_grad, total,
        ins=[None] * 2 + [pl.ANY],
        out_space=hbm,
        scratch=[vmem((padded, width), bf16), dma((BLOCKS,))],
    )
    returned = lax.all_to_all(back.reshape(peers, cap, width), "expert", split_axis=0, concat_axis=0, tiled=True)
    for t in range(1, n + 1):
        total = along(total, FAN)
        if t == TIE:
            total, returned = lax.optimization_barrier((total, returned))
        total = total.astype(f32) + terms[n - t]
        total = total.astype(bf16) if t < n else total
    low, high = total[:rows], total[rows:]
    other = swap(jnp.where(core == 0, high, low).astype(bf16))
    summed = (jnp.where(core == 0, low, high) + other.astype(f32)) / jnp.sqrt(f32(groups * slots))

    token_grad = call(
        functools.partial(combine_kernel, peers, cap, slots),
        [((tok_dev, width), bf16)],
        returned.reshape(padded, width), routes_t, count,
    )
    return token_grad, summed[None, :, :ff], summed[None, :, ff:]


def solution(mesh):
    return jax.shard_map(
        on_device,
        mesh=mesh,
        in_specs=(
            P(("dp", "expert"), None),
            P("expert", None, None),
            P("expert", None, None),
            P("dp", "expert", None, None),
            P("dp", "expert", None),
            P(("dp", "expert"), None),
            P(("dp", "expert")),
        ),
        out_specs=(P(("dp", "expert"), None), P("expert", "dp", None), P("expert", "dp", None)),
        check_vma=False,
    )
```

```python
import functools

import jax
import jax.numpy as jnp
from jax import lax
from jax.experimental import pallas as pl
from jax.experimental.pallas import tpu as pltpu
from jax.sharding import PartitionSpec as P

FAN = 4
TIE = 4
BLOCKS = 8


def iota(shape, dim):
    return lax.broadcasted_iota(jnp.int32, shape, dim)


def place_rows(member, cap):
    n, m = member.shape
    ones = member.astype(jnp.float32).astype(jnp.bfloat16)
    before = (iota((m, m), 0) < iota((m, m), 1)).astype(jnp.float32).astype(jnp.bfloat16)
    rank = jnp.dot(ones, before, preferred_element_type=jnp.float32)
    rank = jnp.where(member, rank, -1.0).astype(jnp.int32)
    marks = rank[:, None, :] == iota((n, cap, m), 1)
    return marks.astype(jnp.float32).reshape(n * cap, m).astype(jnp.bfloat16)


def token_marks(routes, count, experts, cap, slots):
    depth, tokens = routes.shape
    rows = iota((experts, tokens), 0)
    member = jnp.zeros((experts, tokens), jnp.int32)
    for r in range(depth):
        owner = jnp.where(count > r, lax.div(routes[r : r + 1], jnp.int32(slots)), -1)
        member = member + (owner == rows).astype(jnp.int32)
    return place_rows(member > 0, cap)


def slot_marks(chosen, sources, cap, tokens):
    source = lax.div(chosen, jnp.int32(tokens))
    return place_rows(source == iota((sources, chosen.shape[1]), 0), cap)


def contract(a, b, dims):
    return lax.dot_general(a, b, (dims, ((), ())), preferred_element_type=jnp.float32)


def fetch(pairs, sems):
    copies = [pltpu.make_async_copy(src, dst, sems.at[i]) for i, (src, dst) in enumerate(pairs)]
    for copy in copies:
        copy.start()
    return copies


def marked_rows(marks, rows, out_ref, stage_ref, sems):
    size = marks.shape[0] // BLOCKS
    copies = []
    for i in range(BLOCKS):
        span = pl.ds(i * size, size)
        block = jnp.dot(marks[i * size : (i + 1) * size], rows, preferred_element_type=jnp.float32)
        stage_ref[span] = block.astype(jnp.bfloat16)
        copies.append(pltpu.make_async_copy(stage_ref.at[span], out_ref.at[span], sems.at[i]))
        copies[-1].start()
    for copy in copies:
        copy.wait()


def dispatch_kernel(experts, cap, slots, tokens_hbm, routes_hbm, count_hbm, out_ref, tokens_ref, routes_ref, count_ref, stage_ref, in_sems, out_sems):
    tokens_in, routes_in, count_in = fetch(
        [(tokens_hbm, tokens_ref), (routes_hbm, routes_ref), (count_hbm, count_ref)], in_sems
    )
    routes_in.wait()
    count_in.wait()
    marks = token_marks(routes_ref[...], count_ref[...], experts, cap, slots)
    tokens_in.wait()
    marked_rows(marks, tokens_ref[...], out_ref, stage_ref, out_sems)


def combine_kernel(experts, cap, slots, back_ref, routes_ref, count_ref, out_ref):
    marks = token_marks(routes_ref[...], count_ref[...], experts, cap, slots)
    out_ref[...] = contract(marks, back_ref[...], ((0,), (0,))).astype(jnp.bfloat16)


def delta_kernel(sources, cap, tokens, arrived_ref, chosen_ref, order_ref, gate_hbm, up_hbm, grad_hbm, mine_ref, send_ref, gate_ref, up_ref, grad_ref, sems):
    ff = gate_ref.shape[1]
    width = arrived_ref.shape[1]
    half = width // 2
    top, low = pl.ds(0, half), pl.ds(half, half)
    gate_in, gate_too, up_in, up_too, grad_in = fetch(
        [(w.at[part], v.at[part]) for w, v in ((gate_hbm, gate_ref), (up_hbm, up_ref)) for part in (top, low)]
        + [(grad_hbm, grad_ref)],
        sems,
    )
    marks = slot_marks(chosen_ref[...], sources, cap, tokens)
    rows = contract(marks, arrived_ref[...], ((0,), (0,))).astype(jnp.bfloat16)
    pick = (iota((width, width), 0) == order_ref[...]).astype(jnp.float32).astype(jnp.bfloat16)
    ordered = jnp.dot(rows, pick, preferred_element_type=jnp.float32).astype(jnp.bfloat16)
    mine_ref[...] = ordered[:, :half]
    send_ref[:, :half] = ordered[:, half:]
    gate_in.wait()
    gate_too.wait()
    gate = jnp.dot(rows, gate_ref[...], preferred_element_type=jnp.float32)
    up_in.wait()
    up_too.wait()
    up = jnp.dot(rows, up_ref[...], preferred_element_type=jnp.float32)
    squash = jax.nn.sigmoid(gate)
    grad_in.wait()
    upstream = grad_ref[...].astype(jnp.float32)
    send_ref[:, half : half + ff] = (upstream * up * (squash * (1.0 + gate * (1.0 - squash)))).astype(jnp.bfloat16)
    send_ref[:, half + ff :] = (upstream * (gate * squash)).astype(jnp.bfloat16)


def slot_grad_kernel(half, send_ref, gate_hbm, up_hbm, out_ref, gate_ref, up_ref, sems):
    ff = gate_ref.shape[1]
    gate_in, up_in = fetch([(gate_hbm, gate_ref), (up_hbm, up_ref)], sems)
    gate_in.wait()
    grad = contract(send_ref[:, half : half + ff], gate_ref[...], ((1,), (1,)))
    up_in.wait()
    grad = grad + contract(send_ref[:, half + ff :], up_ref[...], ((1,), (1,)))
    out_ref[...] = grad.astype(jnp.bfloat16)


def back_kernel(sources, cap, tokens, chosen_ref, grad_ref, after_ref, out_ref, stage_ref, sems):
    del after_ref
    marks = slot_marks(chosen_ref[...], sources, cap, tokens)
    marked_rows(marks, grad_ref[...], out_ref, stage_ref, sems)


def weight_kernel(mine_ref, send_ref, got_ref, after_ref, keep_ref, next_ref, past_ref, far_ref):
    del after_ref
    half = mine_ref.shape[1]
    block = half // FAN

    def part(q):
        cols = slice(q * block, (q + 1) * block)
        own = contract(mine_ref[:, cols], send_ref[:, half:], ((0,), (0,)))
        return own + contract(got_ref[:, cols], got_ref[:, half:], ((0,), (0,)))

    far_ref[...] = part(2).astype(jnp.bfloat16)
    next_ref[...] = part(1).astype(jnp.bfloat16)
    past_ref[...] = part(3).astype(jnp.bfloat16)
    keep_ref[...] = part(0)


def call(kernel, outs, *args, ins=None, out_space=None, scratch=(), mib=40):
    shapes = [jax.ShapeDtypeStruct(*o) for o in outs]
    spaces = [s or pltpu.VMEM for s in (ins or [None] * len(args))]
    out_specs = [pl.BlockSpec(memory_space=out_space or pltpu.VMEM) for _ in shapes]
    return pl.pallas_call(
        kernel,
        in_specs=[pl.BlockSpec(memory_space=s) for s in spaces],
        out_specs=out_specs if len(shapes) > 1 else out_specs[0],
        out_shape=shapes if len(shapes) > 1 else shapes[0],
        scratch_shapes=list(scratch),
        compiler_params=pltpu.CompilerParams(vmem_limit_bytes=mib * 2**20),
    )(*args)


def on_device(tokens, gate_weight, up_weight, hidden_grad, chosen, routes, route_count):
    tok_dev, width = tokens.shape
    slots, ff = hidden_grad.shape[2:]
    peers = lax.axis_size("expert")
    groups = lax.axis_size("dp")
    cap = min(tok_dev, 2 * slots // peers)
    chips = groups // 2
    rows = width // groups
    half = width // 2
    bf16, f32 = jnp.bfloat16, jnp.float32
    place = lax.axis_index("dp")
    z, core = place // 2, place % 2

    def along(value, hops):
        pairs = [(d, ((d // 2 + (hops if d % 2 == 0 else -hops)) % chips) * 2 + d % 2) for d in range(groups)]
        return lax.ppermute(value, "dp", pairs)

    def swap(value):
        return lax.ppermute(value, "dp", [(d, d ^ 1) for d in range(groups)])

    n = chips // 2 // FAN
    routes_t = routes.T
    count = route_count[None, :]
    picked = chosen[0]
    gate, up = gate_weight[0], up_weight[0]
    hbm, vmem, dma = pltpu.HBM, pltpu.VMEM, pltpu.SemaphoreType.DMA
    padded = peers * cap

    outgoing = call(
        functools.partial(dispatch_kernel, peers, cap, slots),
        [((padded, width), bf16)],
        tokens, routes_t, count,
        ins=[hbm] * 3,
        out_space=hbm,
        scratch=[
            vmem(tokens.shape, bf16), vmem(routes_t.shape, jnp.int32), vmem(count.shape, jnp.int32),
            vmem((padded, width), bf16), dma((3,)), dma((BLOCKS,)),
        ],
        mib=61,
    )
    arrived = lax.all_to_all(
        outgoing.reshape(peers, cap, width), "expert", split_axis=0, concat_axis=0, tiled=True
    ).reshape(padded, width)

    m = jnp.arange(width, dtype=jnp.int32)
    block = half // FAN
    which, q, i = m // half, (m % half) // block, (m % block) // (2 * rows)
    to_core = jnp.where(which == 0, core, 1 - core)
    first = jnp.where(q == 0, jnp.where(to_core == 0, chips // 2, 0), chips // 2 - 1)
    ahead = jnp.where((q == 1) | (q == 2), FAN * i + q, jnp.where(i == 0, first, FAN * i - jnp.where(q == 0, 0, 1)))
    owner = (z + jnp.where(to_core == 0, ahead, -ahead) + chips) % chips
    order = (owner * 2 * rows + m % (2 * rows))[None, :]
    mine, send = call(
        functools.partial(delta_kernel, peers, cap, tok_dev),
        [((slots, half), bf16), ((slots, half + 2 * ff), bf16)],
        arrived, picked, order, gate, up, hidden_grad[0, 0],
        ins=[None] * 3 + [hbm] * 3,
        scratch=[vmem(a.shape, bf16) for a in (gate, up, hidden_grad[0, 0])] + [dma((5,))],
        mib=50,
    )
    got = swap(send)
    slot_grad = call(
        functools.partial(slot_grad_kernel, half),
        [((slots, width), bf16)],
        send, gate, up,
        ins=[None] + [hbm] * 2,
        scratch=[vmem(gate.shape, bf16), vmem(up.shape, bf16), dma((2,))],
        mib=50,
    )
    keep, to_1, to_past, to_2 = call(
        weight_kernel,
        [((block, 2 * ff), f32)] + [((block, 2 * ff), bf16)] * 3,
        mine, send, got, slot_grad,
        ins=[None] * 3 + [pl.ANY],
        mib=40,
    )
    from_past, from_1, from_2 = along(to_past, -1), along(to_1, 1), along(to_2, 2)
    piece = 2 * rows
    total = (from_past[:piece].astype(f32) + jnp.where(core == 0, keep[:piece], 0.0)).astype(bf16)
    inner = jnp.arange(block)[:, None] >= piece
    terms = jnp.where(inner, keep + from_past.astype(f32), jnp.where(core == 1, keep, 0.0))
    terms = terms + from_1.astype(f32) + from_2.astype(f32)
    terms = lax.optimization_barrier(terms).reshape(n, piece, 2 * ff)
    back = call(
        functools.partial(back_kernel, peers, cap, tok_dev),
        [((padded, width), bf16)],
        picked, slot_grad, total,
        ins=[None] * 2 + [pl.ANY],
        out_space=hbm,
        scratch=[vmem((padded, width), bf16), dma((BLOCKS,))],
    )
    returned = lax.all_to_all(back.reshape(peers, cap, width), "expert", split_axis=0, concat_axis=0, tiled=True)
    for t in range(1, n + 1):
        total = along(total, FAN)
        if t == TIE:
            total, returned = lax.optimization_barrier((total, returned))
        total = total.astype(f32) + terms[n - t]
        total = total.astype(bf16) if t < n else total
    low, high = total[:rows], total[rows:]
    other = swap(jnp.where(core == 0, high, low).astype(bf16))
    summed = (jnp.where(core == 0, low, high) + other.astype(f32)) / jnp.sqrt(f32(groups * slots))

    token_grad = call(
        functools.partial(combine_kernel, peers, cap, slots),
        [((tok_dev, width), bf16)],
        returned.reshape(padded, width), routes_t, count,
    )
    return token_grad, summed[None, :, :ff], summed[None, :, ff:]


def solution(mesh):
    return jax.shard_map(
        on_device,
        mesh=mesh,
        in_specs=(
            P(("dp", "expert"), None),
            P("expert", None, None),
            P("expert", None, None),
            P("dp", "expert", None, None),
            P("dp", "expert", None),
            P(("dp", "expert"), None),
            P(("dp", "expert")),
        ),
        out_specs=(P(("dp", "expert"), None), P("expert", "dp", None), P("expert", "dp", None)),
        check_vma=False,
    )
```
